32 devices in a mesh: row: 4 (over z), col: 8 (over y, x, core).
Axes of the slice: x: 2, y: 2, z: 4, core: 2. Of those that a mesh axis runs over, the one named last changes fastest.
Arguments:
- features: bfloat16 [4096, 256], P(('col', 'row')), may hold values from -6 to 6
- weight: bfloat16 [256, 256], replicated, may hold values from -0.375 to 0.375
- bias: float32 [256], replicated, may hold values from -3 to 3
- grad_out: bfloat16 [4096, 256], P(('row', 'col')), may hold values from -6 to 6
- tile_rows: int32 [4, 8, 128], P('row', 'col'), may hold values from 0 to 7
- tile_cols: int32 [4, 8, 128], P('row', 'col'), may hold values from 0 to 3
- tile_counts: int32 [4, 8], P('row', 'col'), may hold values from 1 to 128, as said below
- tile_values: bfloat16 [4, 8, 128, 128, 128], P('row', 'col'), may hold values from 0 to 0.011962891
Outputs:
- output: bfloat16 [4096, 256], P(('row', 'col'))
- grad_features: bfloat16 [4096, 256], P(('col', 'row'))
- grad_weight: float32 [256, 256], replicated
- grad_bias: float32 [256], replicated
The draws below stay inside these ranges and needn't reach their ends.
Inputs may be any that keep to these rules, and one draw needn't show every extreme that they name: `tile_counts`: some grid cell has all 128 slots live. Tile coordinates may repeat within a cell; repeated tiles add.
All inputs are finite; a program needn't handle non-finite values.
Results may differ from the reference program's by a relative error of at most 0.018.
Values may be sent and summed in bfloat16 or wider, within the bound.
A program may use at most 64 MiB of HBM per device.

```python
import jax
import jax.numpy as jnp
from jax import lax

C = 256
TILE = 128
SLOTS = 128
VERTICES = 4096
ROW_TILES = 8
COL_TILES = 4
N_ROW = 4
N_COL = 8


def draw_tile_counts(key, part):
    cells = N_ROW * N_COL
    base = jax.random.randint(jax.random.fold_in(key, 11), (cells,), SLOTS // 8, SLOTS // 2 + 1)
    picks = jax.random.randint(jax.random.fold_in(key, 12), (cells,), 0, 16)
    filled = jnp.where(picks == 0, SLOTS, base)
    chosen = jax.random.randint(jax.random.fold_in(key, 13), (), 0, cells)
    filled = jnp.where(jnp.arange(cells) == chosen, SLOTS, filled)
    return filled.reshape(N_ROW, N_COL).astype(jnp.int32)


def plant(values, rng, low, largest):
    shape = values.shape
    index_at = [jax.random.randint(jax.random.fold_in(rng, axis), (), 0, shape[axis]) for axis in range(len(shape))]
    values = values.at[tuple(index_at)].set(low)
    longest = shape.index(max(shape))
    index_at[longest] = (index_at[longest] + 1) % shape[longest]
    return values.at[tuple(index_at)].set(largest)


def block_scale(key, shape, pieces, smallest, top_value):
    gain, own = 1.0, jax.random.fold_in(key, 6)
    for axis_at, parts in pieces:
        steps = jnp.exp(jax.random.uniform(jax.random.fold_in(own, axis_at), (parts,), jnp.float32, smallest / len(pieces), top_value / len(pieces)))
        gain = gain * jnp.repeat(steps, shape[axis_at] // parts).reshape([-1 if axis == axis_at else 1 for axis in range(len(shape))])
    return gain


def gaussian(stream_key, dims, deviation, most, cuts=(), held_as=jnp.bfloat16):
    values = deviation * jax.random.normal(stream_key, dims, jnp.float32)
    if cuts:
        values = values * block_scale(stream_key, dims, cuts, -0.22, 0.18)
    return jnp.clip(values, -most, most).astype(held_as)


def setup_inputs(seed: int = 0) -> dict:
    splits = jax.random.split(jax.random.key(seed), 9)
    features = gaussian(splits[0], (VERTICES, C), 1.0, 6.0, ((0, 32),))
    weight = gaussian(splits[1], (C, C), C ** -0.5, 0.375)
    bias = gaussian(splits[2], (C,), 0.5, 3.0, (), jnp.float32)
    grad_out = gaussian(splits[3], (VERTICES, C), 1.0, 6.0, ((0, 32),))
    tile_rows = plant(jax.random.randint(splits[4], (N_ROW, N_COL, SLOTS), 0, ROW_TILES), jax.random.fold_in(splits[4], 1), 0, ROW_TILES - 1).astype(jnp.int32)
    tile_cols = plant(jax.random.randint(splits[5], (N_ROW, N_COL, SLOTS), 0, COL_TILES), jax.random.fold_in(splits[5], 1), 0, COL_TILES - 1).astype(jnp.int32)
    tile_counts = draw_tile_counts(jax.random.fold_in(splits[8], 71), 0)
    tile_values = jnp.clip(0.011962891 * jax.random.uniform(splits[7], (N_ROW, N_COL, SLOTS, TILE, TILE), jnp.float32) ** block_scale(splits[7], (N_ROW, N_COL, SLOTS, TILE, TILE), ((0, 4), (1, 8)), -0.2, 0.2), 0.0, 0.011962891).astype(jnp.bfloat16)
    return dict(features=features, weight=weight, bias=bias, grad_out=grad_out, tile_rows=tile_rows, tile_cols=tile_cols, tile_counts=tile_counts, tile_values=tile_values)


def elu_value(pre):
    return jnp.where(pre > 0, pre, jnp.expm1(jnp.minimum(pre, 0.0)))


def elu_slope(pre):
    return jnp.where(pre > 0, jnp.float32(1.0), jnp.exp(jnp.minimum(pre, 0.0)))


def cell_terms(values, dest_idx, src_idx, live, source, dest_tiles, transpose):
    blocks = source[src_idx]
    if transpose:
        prod = jnp.einsum("gab,gac->gbc", values.astype(jnp.float32), blocks.astype(jnp.float32))
    else:
        prod = jnp.einsum("gab,gbc->gac", values.astype(jnp.float32), blocks.astype(jnp.float32))
    keep = (jnp.arange(values.shape[0]) < live).astype(jnp.float32)
    onehot = (dest_idx[None, :] == jnp.arange(dest_tiles)[:, None]).astype(jnp.float32) * keep[None, :]
    return jnp.einsum("kg,gac->kac", onehot, prod, precision=lax.Precision.HIGHEST)


def reference(features, weight, bias, grad_out, tile_rows, tile_cols, tile_counts, tile_values):
    mixed = jnp.dot(features, weight, preferred_element_type=jnp.float32).astype(jnp.bfloat16)
    mixed_blocks = mixed.reshape(N_COL, COL_TILES, TILE, C)

    def forward_row(i):
        def add_cell(j, acc):
            return acc + cell_terms(tile_values[i, j], tile_rows[i, j], tile_cols[i, j], tile_counts[i, j], mixed_blocks[j], ROW_TILES, False)
        return lax.fori_loop(0, N_COL, add_cell, jnp.zeros((ROW_TILES, TILE, C), jnp.float32))

    aggregate = lax.map(forward_row, jnp.arange(N_ROW))
    pre = aggregate.reshape(VERTICES, C) + bias[None, :]
    output = elu_value(pre).astype(jnp.bfloat16)
    grad_pre = (grad_out.astype(jnp.float32) * elu_slope(pre)).astype(jnp.bfloat16)
    grad_blocks = grad_pre.reshape(N_ROW, ROW_TILES, TILE, C)

    def backward_col(j):
        def add_cell(i, acc):
            return acc + cell_terms(tile_values[i, j], tile_cols[i, j], tile_rows[i, j], tile_counts[i, j], grad_blocks[i], COL_TILES, True)
        return lax.fori_loop(0, N_ROW, add_cell, jnp.zeros((COL_TILES, TILE, C), jnp.float32))

    grad_mixed = lax.map(backward_col, jnp.arange(N_COL)).reshape(VERTICES, C).astype(jnp.bfloat16)
    grad_features = jnp.dot(grad_mixed, weight.T, preferred_element_type=jnp.float32).astype(jnp.bfloat16)
    grad_weight = jnp.dot(features.T, grad_mixed, preferred_element_type=jnp.float32)
    grad_bias = jnp.sum(grad_pre.astype(jnp.float32), axis=0)
    return (output, grad_features, grad_weight, grad_bias)
```

```python
import functools

import jax
import jax.numpy as jnp
from jax import lax
from jax.experimental import pallas as pl
from jax.experimental.pallas import tpu as pltpu
from jax.sharding import PartitionSpec as P

MESH = pl.DeviceIdType.MESH
CHUNKS = 4
F32 = jnp.float32
BF16 = jnp.bfloat16


def each(n, step):
    if n <= 8:
        for i in range(n):
            step(i)
    else:
        lax.fori_loop(0, n, lambda i, _: (step(i), 0)[1], 0)


def kernel(
    n_row, n_col, row_tiles, col_tiles,
    feat_ref, weight_ref, bias_ref, gout_ref, rows_ref, cols_ref, count_ref, values_ref,
    out_ref, gfeat_ref, gw_ref, gb_ref,
    vals, seq, dense, dense_t, feat_all, feat_t, mixed, part_send, part_recv, grad_all,
    back_send, back_recv, gw_send, gw_recv, gwz_recv, gw_all, gb_recv, idx_v, idx_s,
    val_sem, idx_sem, f_send, f_recv, p_send, p_recv, g_send, g_recv, b_send, b_recv,
    w_send, w_recv, z_send, z_recv, a_send, a_recv, s_send, s_recv,
):
    my_r = lax.axis_index("row")
    my_c = lax.axis_index("col")
    slots, side = vals.shape[0], vals.shape[1]
    share, width = feat_ref.shape
    per = slots // CHUNKS
    chunk = width // n_col

    def row_peer(d):
        return lax.rem(my_r + d, n_row)

    def row_from(d):
        return lax.rem(my_r + n_row - d, n_row)

    def col_peer(d):
        return lax.rem(my_c + d, n_col)

    def col_from(d):
        return lax.rem(my_c + n_col - d, n_col)

    def to_row(src, dst, send, recv, d):
        return pltpu.make_async_remote_copy(
            src_ref=src, dst_ref=dst, send_sem=send.at[d], recv_sem=recv.at[d],
            device_id=(row_peer(d), my_c), device_id_type=MESH)

    def to_col(src, dst, send, recv, d):
        return pltpu.make_async_remote_copy(
            src_ref=src, dst_ref=dst, send_sem=send.at[d], recv_sem=recv.at[d],
            device_id=(my_r, col_peer(d)), device_id_type=MESH)

    def fetch(q):
        return pltpu.make_async_copy(
            values_ref.at[pl.ds(q * per, per)], vals.at[pl.ds(q * per, per)], val_sem.at[q])

    for q in range(CHUNKS):
        fetch(q).start()

    barrier = pltpu.get_barrier_semaphore()
    for d in range(1, n_row):
        pl.semaphore_signal(barrier, inc=1, device_id=(row_peer(d), my_c), device_id_type=MESH)
    for d in range(1, n_col):
        pl.semaphore_signal(barrier, inc=1, device_id=(my_r, col_peer(d)), device_id_type=MESH)

    tiles = row_tiles * col_tiles
    lane = lax.broadcasted_iota(jnp.int32, (slots, slots), 1)
    sub = lax.broadcasted_iota(jnp.int32, (slots, slots), 0)
    live = lane < count_ref[0, 0]
    key = jnp.where(
        live, jnp.broadcast_to(rows_ref[...] * col_tiles + cols_ref[...], (slots, slots)), tiles)
    key_t = key.T
    ahead = (key_t < key) | ((key_t == key) & (sub < lane))
    rank = jnp.sum(ahead.astype(jnp.int32), axis=0, keepdims=True)
    hit = jnp.broadcast_to(rank, (slots, slots)).T == lane
    idx_v[0:1, :] = jnp.sum(jnp.where(hit, sub, 0), axis=0, keepdims=True)
    idx_v[1:2, :] = jnp.sum(jnp.where(hit, key_t, 0), axis=0, keepdims=True)
    for q in range(-(-tiles // slots)):
        upto = (key_t <= lane + q * slots).astype(jnp.int32)
        idx_v[2 + q : 3 + q, :] = jnp.sum(upto, axis=0, keepdims=True)
    idx_copy = pltpu.make_async_copy(idx_v, idx_s, idx_sem)
    idx_copy.start()

    pl.semaphore_wait(barrier, n_row + n_col - 2)

    def feat_copy(d):
        return to_row(feat_ref, feat_all.at[my_r], f_send, f_recv, d)

    for d in range(1, n_row):
        feat_copy(d).start()
    feat_all[my_r] = feat_ref[...]

    idx_copy.wait()
    for q in range(CHUNKS):
        fetch(q).wait()

    def add_slot(i, acc):
        same = (i > 0) & (idx_s[1, i] == idx_s[1, jnp.maximum(i - 1, 0)])
        keep = jnp.where(same, 1.0, 0.0).astype(F32)
        acc = acc * keep + vals[idx_s[0, i]].astype(F32)
        seq[i] = acc.astype(BF16)
        return acc

    lax.fori_loop(0, slots, add_slot, jnp.zeros((side, side), F32), unroll=4)

    def dense_tile(r, c):
        k = r * col_tiles + c
        before = jnp.maximum(k - 1, 0)
        end = idx_s[2 + k // slots, lax.rem(k, slots)]
        start = jnp.where(k > 0, idx_s[2 + before // slots, lax.rem(before, slots)], 0)
        some = jnp.where(end > start, 1.0, 0.0).astype(F32)
        return (seq[jnp.maximum(end - 1, 0)].astype(F32) * some).astype(BF16)

    def place(r, _):
        for c in range(col_tiles):
            dense[pl.ds(pl.multiple_of(r * side, side), side), c * side : (c + 1) * side] = (
                dense_tile(r, c))
        return 0

    lax.fori_loop(0, row_tiles, place, 0)

    def mix(i):
        mixed[pl.ds(i * share, share), :] = jnp.dot(
            feat_all[i], weight_ref[...], preferred_element_type=F32).astype(BF16)

    mix(my_r)

    for d in range(1, n_row):
        feat_copy(d).wait_recv()
        mix(row_from(d))

    def part_copy(d):
        return to_col(part_send.at[d], part_recv.at[d], p_send, p_recv, d)

    def forward(j):
        return jnp.dot(
            dense[pl.ds(pl.multiple_of(j * share, share), share), :], mixed[...],
            preferred_element_type=F32)

    def forward_send(i):
        d = i + 1
        part_send[d] = forward(col_peer(d)).astype(BF16)
        part_copy(d).start()

    each(n_col - 1, forward_send)
    pre = forward(my_c) + bias_ref[...]

    def turn(r, _):
        for c in range(col_tiles):
            tile = dense[pl.ds(pl.multiple_of(r * side, side), side), c * side : (c + 1) * side]
            dense_t[c * side : (c + 1) * side, pl.ds(pl.multiple_of(r * side, side), side)] = (
                tile.astype(F32).T.astype(BF16))
        return 0

    lax.fori_loop(0, row_tiles, turn, 0)

    def turn_feat(i, _):
        feat_t[:, pl.ds(pl.multiple_of(i * share, share), share)] = (
            feat_all[i].astype(F32).T.astype(BF16))
        return 0

    lax.fori_loop(0, n_row, turn_feat, 0)

    for d in range(1, n_col):
        part_copy(d).wait_recv()
        pre = pre + part_recv[d].astype(F32)

    low = jnp.exp(jnp.minimum(pre, 0.0))
    grad = (gout_ref[...].astype(F32) * jnp.where(pre > 0, 1.0, low)).astype(BF16)
    my_rows = pl.ds(pl.multiple_of(my_c * share, share), share)
    grad_all[my_rows, :] = grad

    def grad_copy(d):
        return to_col(grad_all.at[my_rows], grad_all.at[my_rows], g_send, g_recv, d)

    for d in range(1, n_col):
        grad_copy(d).start()
    out_ref[...] = jnp.where(pre > 0, pre, low - 1.0).astype(BF16)
    for d in range(1, n_col):
        grad_copy(d).wait_recv()

    def back_copy(d):
        return to_row(back_send.at[row_peer(d)], back_recv.at[d], b_send, b_recv, d)

    def backward(i):
        return jnp.dot(
            dense_t[pl.ds(pl.multiple_of(i * share, share), share), :], grad_all[...],
            preferred_element_type=F32)

    def backward_send(i):
        d = i + 1
        back_send[row_peer(d)] = backward(row_peer(d)).astype(BF16)
        back_copy(d).start()

    each(n_row - 1, backward_send)
    total = backward(my_r)
    back_send[my_r] = total.astype(BF16)

    def gw_copy(d):
        return to_col(gw_send.at[col_peer(d)], gw_recv.at[d], w_send, w_recv, d)

    term = jnp.dot(
        feat_t[...], back_send[...].reshape(n_row * share, width), preferred_element_type=F32)
    gw_send[...] = term.astype(gw_send.dtype).reshape(n_col, chunk, width)
    for d in range(1, n_col):
        gw_copy(d).start()

    def gb_copy(d):
        return to_row(gb_recv.at[my_r], gb_recv.at[my_r], s_send, s_recv, d)

    ones = jnp.ones((16, n_col * share), BF16)
    gb_recv[my_r] = jnp.dot(ones, grad_all[...], preferred_element_type=F32)[:8]
    for d in range(1, n_row):
        gb_copy(d).start()

    gw_sum = gw_send[my_c].astype(F32)
    for d in range(1, n_col):
        gw_copy(d).wait_recv()
        gw_sum = gw_sum + gw_recv[d].astype(F32)

    def gwz_copy(d):
        return to_row(gwz_recv.at[my_r], gwz_recv.at[my_r], z_send, z_recv, d)

    gwz_recv[my_r] = gw_sum.astype(gw_send.dtype)
    for d in range(1, n_row):
        gwz_copy(d).start()

    for d in range(1, n_row):
        back_copy(d).wait_recv()
        total = total + back_recv[d].astype(F32)
    gfeat_ref[...] = lax.dot_general(
        total.astype(BF16), weight_ref[...], (((1,), (1,)), ((), ())),
        preferred_element_type=F32).astype(BF16)

    for d in range(1, n_row):
        gwz_copy(d).wait_recv()
    whole = gwz_recv[0].astype(F32)
    for i in range(1, n_row):
        whole = whole + gwz_recv[i].astype(F32)

    def all_copy(d):
        return to_col(gw_all.at[my_c], gw_all.at[my_c], a_send, a_recv, d)

    gw_all[my_c] = whole.astype(gw_all.dtype)
    for d in range(1, n_col):
        all_copy(d).start()

    for d in range(1, n_row):
        gb_copy(d).wait_recv()
    gb = gb_recv[0]
    for i in range(1, n_row):
        gb = gb + gb_recv[i]
    gb_ref[...] = gb[0:1]

    for d in range(1, n_row):
        feat_copy(d).wait_send()
        back_copy(d).wait_send()
        gwz_copy(d).wait_send()
        gb_copy(d).wait_send()
    for d in range(1, n_col):
        part_copy(d).wait_send()
        grad_copy(d).wait_send()
        gw_copy(d).wait_send()
    for d in range(1, n_col):
        all_copy(d).wait_recv()
    gw_ref[...] = gw_all[...].astype(F32).reshape(width, width)
    for d in range(1, n_col):
        all_copy(d).wait_send()


def body(n_row, n_col, features, weight, bias, grad_out, tile_rows, tile_cols, tile_counts, tile_values):
    values = tile_values[0, 0]
    slots, side = values.shape[0], values.shape[1]
    share, width = features.shape
    row_tiles = share * n_col // side
    col_tiles = share * n_row // side
    chunk = width // n_col
    gw_type = BF16 if chunk % 16 == 0 else F32
    index_rows = -(-(2 + -(-(row_tiles * col_tiles) // slots)) // 8) * 8
    vmem = pl.BlockSpec(memory_space=pltpu.VMEM)
    smem = pl.BlockSpec(memory_space=pltpu.SMEM)
    dma = pltpu.SemaphoreType.DMA
    row_sem, col_sem = dma((n_row,)), dma((n_col,))
    out, gfeat, gw, gb = pl.pallas_call(
        functools.partial(kernel, n_row, n_col, row_tiles, col_tiles),
        out_shape=(
            jax.ShapeDtypeStruct((share, width), BF16),
            jax.ShapeDtypeStruct((share, width), BF16),
            jax.ShapeDtypeStruct((width, width), F32),
            jax.ShapeDtypeStruct((1, width), F32),
        ),
        in_specs=[vmem] * 6 + [smem, pl.BlockSpec(memory_space=pl.ANY)],
        out_specs=(vmem, vmem, vmem, vmem),
        scratch_shapes=[
            pltpu.VMEM((slots, side, side), BF16),
            pltpu.VMEM((slots, side, side), BF16),
            pltpu.VMEM((row_tiles * side, col_tiles * side), BF16),
            pltpu.VMEM((col_tiles * side, row_tiles * side), BF16),
            pltpu.VMEM((n_row, share, width), BF16),
            pltpu.VMEM((width, n_row * share), BF16),
            pltpu.VMEM((n_row * share, width), BF16),
            pltpu.VMEM((n_col, share, width), BF16),
            pltpu.VMEM((n_col, share, width), BF16),
            pltpu.VMEM((n_col * share, width), BF16),
            pltpu.VMEM((n_row, share, width), BF16),
            pltpu.VMEM((n_row, share, width), BF16),
            pltpu.VMEM((n_col, chunk, width), gw_type),
            pltpu.VMEM((n_col, chunk, width), gw_type),
            pltpu.VMEM((n_row, chunk, width), gw_type),
            pltpu.VMEM((n_col, chunk, width), gw_type),
            pltpu.VMEM((n_row, 8, width), F32),
            pltpu.VMEM((index_rows, slots), jnp.int32),
            pltpu.SMEM((index_rows, slots), jnp.int32),
            dma((CHUNKS,)), dma(()),
            row_sem, row_sem, col_sem, col_sem, col_sem, col_sem, row_sem, row_sem,
            col_sem, col_sem, row_sem, row_sem, col_sem, col_sem, row_sem, row_sem,
        ],
        compiler_params=pltpu.CompilerParams(
            collective_id=0, has_side_effects=True, vmem_limit_bytes=60 * 2**20),
        cost_estimate=pl.CostEstimate(
            flops=4 * row_tiles * col_tiles * side * side * width,
            bytes_accessed=2 * slots * side * side, transcendentals=share * width),
    )(features, weight, bias[None, :], grad_out, tile_rows[0], tile_cols[0], tile_counts, values)
    return out, gfeat, gw, gb[0]


def solution(mesh):
    placed = (
        P(("col", "row"), None),
        P(),
        P(),
        P(("row", "col"), None),
        P("row", "col", None),
        P("row", "col", None),
        P("row", "col"),
        P("row", "col", None, None, None),
    )
    return jax.shard_map(
        functools.partial(body, mesh.shape["row"], mesh.shape["col"]),
        mesh=mesh,
        in_specs=placed,
        out_specs=(P(("row", "col"), None), P(("col", "row"), None), P(), P()),
        check_vma=False,
    )
```

```python
import functools
import math

import jax
import jax.numpy as jnp
from jax import lax
from jax.experimental import pallas as pl
from jax.experimental.pallas import tpu as pltpu
from jax.sharding import PartitionSpec as P

MESH = pl.DeviceIdType.MESH
CHUNKS = 4
F32 = jnp.float32
BF16 = jnp.bfloat16


def each(n, step):
    if n <= 8:
        for i in range(n):
            step(i)
    else:
        lax.fori_loop(0, n, lambda i, _: (step(i), 0)[1], 0)


def kernel(
    n_row, n_col, row_tiles, col_tiles,
    feat_ref, weight_ref, bias_ref, gout_ref, rows_ref, cols_ref, count_ref, values_ref,
    out_ref, gmix_ref, gw_ref, gb_ref,
    vals, seq, dense, dense_t, feat_all, pair_send, pair_recv, part_send, part_recv, grad_all,
    back_send, back_recv, gw_send, gw_recv, gwz_recv, gw_all, gb_recv, idx_v, idx_s,
    val_sem, idx_sem, f_send, f_recv, p_send, p_recv, q_send, q_recv, g_send, g_recv,
    h_send, h_recv, b_send, b_recv,
    w_send, w_recv, z_send, z_recv, a_send, a_recv, s_send, s_recv,
):
    my_r = lax.axis_index("row")
    my_c = lax.axis_index("col")
    n_chip = n_col // 2
    core, chip = lax.rem(my_c, 2), my_c // 2
    sibling = my_c + 1 - 2 * core
    slots, side = vals.shape[0], vals.shape[1]
    share, width = feat_ref.shape
    per = slots // CHUNKS
    chunk = width // n_col

    def row_peer(d):
        return lax.rem(my_r + d, n_row)

    def col_peer(d):
        return lax.rem(my_c + d, n_col)

    def chip_peer(d):
        return 2 * lax.rem(chip + d, n_chip) + core

    def to_row(src, dst, send, recv, d):
        return pltpu.make_async_remote_copy(
            src_ref=src, dst_ref=dst, send_sem=send.at[d], recv_sem=recv.at[d],
            device_id=(row_peer(d), my_c), device_id_type=MESH)

    def to_col(src, dst, send, recv, d, peer):
        return pltpu.make_async_remote_copy(
            src_ref=src, dst_ref=dst, send_sem=send.at[d], recv_sem=recv.at[d],
            device_id=(my_r, peer), device_id_type=MESH)

    def fetch(q):
        return pltpu.make_async_copy(
            values_ref.at[pl.ds(q * per, per)], vals.at[pl.ds(q * per, per)], val_sem.at[q])

    for q in range(CHUNKS):
        fetch(q).start()

    barrier = pltpu.get_barrier_semaphore()
    for d in range(1, n_row):
        pl.semaphore_signal(barrier, inc=1, device_id=(row_peer(d), my_c), device_id_type=MESH)
    for d in range(1, n_col):
        pl.semaphore_signal(barrier, inc=1, device_id=(my_r, col_peer(d)), device_id_type=MESH)

    tiles = row_tiles * col_tiles
    lane = lax.broadcasted_iota(jnp.int32, (slots, slots), 1)
    sub = lax.broadcasted_iota(jnp.int32, (slots, slots), 0)
    live = lane < count_ref[0, 0]
    key = jnp.where(
        live, jnp.broadcast_to(rows_ref[...] * col_tiles + cols_ref[...], (slots, slots)), tiles)
    key_t = key.T
    ahead = (key_t < key) | ((key_t == key) & (sub < lane))
    rank = jnp.sum(ahead.astype(jnp.int32), axis=0, keepdims=True)
    hit = jnp.broadcast_to(rank, (slots, slots)).T == lane
    idx_v[0:1, :] = jnp.sum(jnp.where(hit, sub, 0), axis=0, keepdims=True)
    idx_v[1:2, :] = jnp.sum(jnp.where(hit, key_t, 0), axis=0, keepdims=True)
    for q in range(-(-tiles // slots)):
        upto = (key_t <= lane + q * slots).astype(jnp.int32)
        idx_v[2 + q : 3 + q, :] = jnp.sum(upto, axis=0, keepdims=True)
    idx_copy = pltpu.make_async_copy(idx_v, idx_s, idx_sem)
    idx_copy.start()

    pl.semaphore_wait(barrier, n_row + n_col - 2)

    def feat_copy(d):
        return to_row(feat_ref, feat_all.at[my_r], f_send, f_recv, d)

    for d in range(1, n_row):
        feat_copy(d).start()
    feat_all[my_r] = feat_ref[...]

    idx_copy.wait()
    for q in range(CHUNKS):
        fetch(q).wait()

    def add_slot(i, acc):
        same = (i > 0) & (idx_s[1, i] == idx_s[1, jnp.maximum(i - 1, 0)])
        keep = jnp.where(same, 1.0, 0.0).astype(F32)
        acc = acc * keep + vals[idx_s[0, i]].astype(F32)
        seq[i] = acc.astype(BF16)
        return acc

    lax.fori_loop(0, slots, add_slot, jnp.zeros((side, side), F32), unroll=8)

    def dense_tile(r, c):
        k = r * col_tiles + c
        before = jnp.maximum(k - 1, 0)
        end = idx_s[2 + k // slots, lax.rem(k, slots)]
        start = jnp.where(k > 0, idx_s[2 + before // slots, lax.rem(before, slots)], 0)
        some = jnp.where(end > start, 1.0, 0.0).astype(F32)
        return (seq[jnp.maximum(end - 1, 0)].astype(F32) * some).astype(BF16)

    tiles_per = share // side

    def place(r, _):
        block, inner = r // tiles_per, lax.rem(r, tiles_per)
        at = (lax.rem(block, 2) * n_chip + block // 2) * tiles_per + inner
        for c in range(col_tiles):
            dense[pl.ds(pl.multiple_of(at * side, side), side), c * side : (c + 1) * side] = (
                dense_tile(r, c))
        return 0

    lax.fori_loop(0, row_tiles, place, 0)

    for d in range(1, n_row):
        feat_copy(d).wait_recv()

    def aggregate(block):
        return jnp.dot(
            dense[pl.ds(pl.multiple_of(block * share, share), share), :],
            feat_all[...].reshape(n_row * share, width), preferred_element_type=F32)

    def pair_copy(d):
        return to_col(pair_send.at[d], pair_recv.at[d], p_send, p_recv, d, sibling)

    def part_copy(d):
        return to_col(part_send.at[d], part_recv.at[d], q_send, q_recv, d, chip_peer(d))

    def pair_step(i):
        d = lax.rem(i + 1, n_chip)
        pair_send[d] = aggregate((1 - core) * n_chip + lax.rem(chip + d, n_chip)).astype(BF16)
        pair_copy(d).start()

    def part_step(i):
        d = i + 1
        mine = aggregate(core * n_chip + lax.rem(chip + d, n_chip))
        pair_copy(d).wait_recv()
        part_send[d] = (mine + pair_recv[d].astype(F32)).astype(BF16)
        part_copy(d).start()

    each(n_chip, pair_step)
    each(n_chip - 1, part_step)
    gathered = aggregate(core * n_chip + chip)
    pair_copy(0).wait_recv()
    gathered = gathered + pair_recv[0].astype(F32)

    def turn(r, _):
        for c in range(col_tiles):
            tile = dense[pl.ds(pl.multiple_of(r * side, side), side), c * side : (c + 1) * side]
            dense_t[c * side : (c + 1) * side, pl.ds(pl.multiple_of(r * side, side), side)] = (
                tile.astype(F32).T.astype(BF16))
        return 0

    lax.fori_loop(0, row_tiles, turn, 0)

    for d in range(1, n_chip):
        part_copy(d).wait_recv()
        gathered = gathered + part_recv[d].astype(F32)

    pre = jnp.dot(
        gathered.astype(BF16), weight_ref[...], preferred_element_type=F32) + bias_ref[...]
    low = jnp.exp(jnp.minimum(pre, 0.0))
    grad = (gout_ref[...].astype(F32) * jnp.where(pre > 0, 1.0, low)).astype(BF16)

    def rows_of(block):
        return grad_all.at[pl.ds(pl.multiple_of(block * share, share), share), :]

    mine_at = core * n_chip + chip
    grad_all[pl.ds(pl.multiple_of(mine_at * share, share), share), :] = grad

    def grad_copy(d):
        return to_col(rows_of(mine_at), rows_of(mine_at), g_send, g_recv, d, chip_peer(d))

    def hand_copy(d):
        at = core * n_chip + lax.rem(chip + n_chip - d, n_chip)
        return to_col(rows_of(at), rows_of(at), h_send, h_recv, d, sibling)

    for d in range(1, n_chip):
        grad_copy(d).start()
    hand_copy(0).start()
    out_ref[...] = jnp.where(pre > 0, pre, low - 1.0).astype(BF16)

    def gw_copy(d):
        return to_col(gw_send.at[col_peer(d)], gw_recv.at[d], w_send, w_recv, d, col_peer(d))

    term = jnp.dot(gathered.T.astype(BF16), grad, preferred_element_type=F32)
    gw_send[...] = term.astype(gw_send.dtype).reshape(n_col, chunk, width)
    for d in range(1, n_col):
        gw_copy(d).start()

    for d in range(1, n_chip):
        grad_copy(d).wait_recv()
        hand_copy(d).start()
    for d in range(n_chip):
        hand_copy(d).wait_recv()

    def back_copy(d):
        return to_row(back_send.at[d], back_recv.at[d], b_send, b_recv, d)

    def backward(i):
        return jnp.dot(
            dense_t[pl.ds(pl.multiple_of(i * share, share), share), :], grad_all[...],
            preferred_element_type=F32)

    def backward_send(i):
        d = i + 1
        back_send[d] = backward(row_peer(d)).astype(BF16)
        back_copy(d).start()

    each(n_row - 1, backward_send)

    gw_sum = gw_send[my_c].astype(F32)
    for d in range(1, n_col):
        gw_copy(d).wait_recv()
        gw_sum = gw_sum + gw_recv[d].astype(F32)

    def gwz_copy(d):
        return to_row(gwz_recv.at[my_r], gwz_recv.at[my_r], z_send, z_recv, d)

    gwz_recv[my_r] = gw_sum.astype(gw_send.dtype)
    for d in range(1, n_row):
        gwz_copy(d).start()

    def gb_copy(d):
        return to_row(gb_recv.at[my_r], gb_recv.at[my_r], s_send, s_recv, d)

    ones = jnp.ones((16, n_col * share), BF16)
    gb_recv[my_r] = jnp.dot(ones, grad_all[...], preferred_element_type=F32)[:8]
    for d in range(1, n_row):
        gb_copy(d).start()

    total = backward(my_r)

    for d in range(1, n_row):
        gwz_copy(d).wait_recv()
    whole = gwz_recv[0].astype(F32)
    for i in range(1, n_row):
        whole = whole + gwz_recv[i].astype(F32)

    def all_copy(d):
        return to_col(gw_all.at[my_c], gw_all.at[my_c], a_send, a_recv, d, col_peer(d))

    gw_all[my_c] = whole.astype(gw_all.dtype)
    for d in range(1, n_col):
        all_copy(d).start()

    for d in range(1, n_row):
        back_copy(d).wait_recv()
        total = total + back_recv[d].astype(F32)
    gmix_ref[...] = total.astype(BF16)

    for d in range(1, n_row):
        gb_copy(d).wait_recv()
    gb_ref[...] = gb_recv[...]

    for d in range(1, n_row):
        feat_copy(d).wait_send()
        back_copy(d).wait_send()
        gwz_copy(d).wait_send()
        gb_copy(d).wait_send()
    for d in range(n_chip):
        pair_copy(d).wait_send()
        hand_copy(d).wait_send()
    for d in range(1, n_chip):
        part_copy(d).wait_send()
        grad_copy(d).wait_send()
    for d in range(1, n_col):
        gw_copy(d).wait_send()
        all_copy(d).wait_recv()
    gw_ref[...] = gw_all[...]
    for d in range(1, n_col):
        all_copy(d).wait_send()


def finish(part_ref, gmix_ref, gwp_ref, gbp_ref, weight_ref, out_ref, gfeat_ref, gw_ref, gb_ref):
    out_ref[...] = part_ref[...]
    gfeat_ref[...] = lax.dot_general(
        gmix_ref[...], weight_ref[...], (((1,), (1,)), ((), ())),
        preferred_element_type=F32).astype(BF16)
    gw_ref[...] = gwp_ref[...].astype(F32).reshape(gw_ref.shape)
    gb = gbp_ref[0]
    for i in range(1, gbp_ref.shape[0]):
        gb = gb + gbp_ref[i]
    gb_ref[...] = gb[0:1]


def body(n_row, n_col, features, weight, bias, grad_out, tile_rows, tile_cols, tile_counts, tile_values):
    values = tile_values[0, 0]
    slots, side = values.shape[0], values.shape[1]
    share, width = features.shape
    row_tiles = share * n_col // side
    col_tiles = share * n_row // side
    chunk = width // n_col
    gw_type = BF16 if chunk % 16 == 0 else F32
    index_rows = -(-(2 + -(-(row_tiles * col_tiles) // slots)) // 8) * 8
    vmem = pl.BlockSpec(memory_space=pltpu.VMEM)
    smem = pl.BlockSpec(memory_space=pltpu.SMEM)
    dma = pltpu.SemaphoreType.DMA
    row_sem, col_sem, chip_sem = dma((n_row,)), dma((n_col,)), dma((n_col // 2,))
    buffers = [
        ((slots, side, side), BF16),
        ((slots, side, side), BF16),
        ((row_tiles * side, col_tiles * side), BF16),
        ((col_tiles * side, row_tiles * side), BF16),
        ((n_row, share, width), BF16),
        ((n_col // 2, share, width), BF16),
        ((n_col // 2, share, width), BF16),
        ((n_col // 2, share, width), BF16),
        ((n_col // 2, share, width), BF16),
        ((n_col * share, width), BF16),
        ((n_row, share, width), BF16),
        ((n_row, share, width), BF16),
        ((n_col, chunk, width), gw_type),
        ((n_col, chunk, width), gw_type),
        ((n_row, chunk, width), gw_type),
        ((n_col, chunk, width), gw_type),
        ((n_row, 8, width), F32),
        ((index_rows, slots), jnp.int32),
    ]
    held = sum(math.prod(shape) * jnp.dtype(kind).itemsize for shape, kind in buffers)
    out, gmix, gw, gb = pl.pallas_call(
        functools.partial(kernel, n_row, n_col, row_tiles, col_tiles),
        out_shape=(
            jax.ShapeDtypeStruct((share, width), BF16),
            jax.ShapeDtypeStruct((share, width), BF16),
            jax.ShapeDtypeStruct((n_col, chunk, width), gw_type),
            jax.ShapeDtypeStruct((n_row, 8, width), F32),
        ),
        in_specs=[vmem] * 6 + [smem, pl.BlockSpec(memory_space=pltpu.HBM)],
        out_specs=(vmem, vmem, vmem, vmem),
        scratch_shapes=[pltpu.VMEM(shape, kind) for shape, kind in buffers] + [
            pltpu.SMEM((index_rows, slots), jnp.int32),
            dma((CHUNKS,)), dma(()),
            row_sem, row_sem, chip_sem, chip_sem, chip_sem, chip_sem, chip_sem, chip_sem,
            chip_sem, chip_sem, row_sem, row_sem,
            col_sem, col_sem, row_sem, row_sem, col_sem, col_sem, row_sem, row_sem,
        ],
        compiler_params=pltpu.CompilerParams(
            collective_id=0, has_side_effects=True,
            vmem_limit_bytes=min(60 * 2**20, held + 12 * 2**20)),
        cost_estimate=pl.CostEstimate(
            flops=4 * row_tiles * col_tiles * side * side * width,
            bytes_accessed=2 * slots * side * side, transcendentals=share * width),
    )(features, weight, bias[None, :], grad_out, tile_rows[0], tile_cols[0], tile_counts, values)
    out, gfeat, gw, gb = pl.pallas_call(
        finish,
        out_shape=(
            jax.ShapeDtypeStruct((share, width), BF16),
            jax.ShapeDtypeStruct((share, width), BF16),
            jax.ShapeDtypeStruct((width, width), F32),
            jax.ShapeDtypeStruct((1, width), F32),
        ),
        in_specs=[vmem] * 5,
        out_specs=(vmem, vmem, vmem, vmem),
    )(out, gmix, gw, gb, weight)
    return out, gfeat, gw, gb[0]


def solution(mesh):
    placed = (
        P(("col", "row"), None),
        P(),
        P(),
        P(("row", "col"), None),
        P("row", "col", None),
        P("row", "col", None),
        P("row", "col"),
        P("row", "col", None, None, None),
    )
    return jax.shard_map(
        functools.partial(body, mesh.shape["row"], mesh.shape["col"]),
        mesh=mesh,
        in_specs=placed,
        out_specs=(P(("row", "col"), None), P(("col", "row"), None), P(), P()),
        check_vma=False,
    )
```

```python
import functools

import jax
import jax.numpy as jnp
from jax import lax
from jax.experimental import pallas as pl
from jax.experimental.pallas import tpu as pltpu
from jax.sharding import PartitionSpec as P

MESH = pl.DeviceIdType.MESH
CHUNKS = 4
VMEM_BYTES = 60 * 2**20
F32 = jnp.float32
BF16 = jnp.bfloat16


def each(n, step):
    if n <= 8:
        for i in range(n):
            step(i)
    else:
        lax.fori_loop(0, n, lambda i, _: (step(i), 0)[1], 0)


def kernel(
    n_row, n_col, row_tiles, col_tiles,
    feat_ref, weight_hbm, bias_hbm, gout_hbm, rows_hbm, cols_hbm, count_ref, values_ref,
    out_hbm, gmix_ref, gw_hbm, gb_hbm,
    weight_ref, bias_ref, gout_ref, rows_ref, cols_ref, out_ref,
    vals, seq, dense, dense_t, feat_all, pair_send, pair_recv, part_send, part_recv, grad_all,
    back_send, back_recv, gw_send, gw_recv, gwz_recv, gw_all, gb_recv, idx_v, idx_s,
    val_sem, idx_sem, in_sem, out_sem, f_send, f_recv, p_send, p_recv, q_send, q_recv, g_send, g_recv,
    h_send, h_recv, b_send, b_recv,
    w_send, w_recv, z_send, z_recv, a_send, a_recv, s_send, s_recv,
):
    my_r = lax.axis_index("row")
    my_c = lax.axis_index("col")
    n_chip = n_col // 2
    core, chip = lax.rem(my_c, 2), my_c // 2
    sibling = my_c + 1 - 2 * core
    slots, side = vals.shape[0], vals.shape[1]
    share, width = feat_ref.shape
    per = slots // CHUNKS
    chunk = width // n_col

    def row_peer(d):
        return lax.rem(my_r + d, n_row)

    def col_peer(d):
        return lax.rem(my_c + d, n_col)

    def chip_peer(d):
        return 2 * lax.rem(chip + d, n_chip) + core

    def to_row(src, dst, send, recv, d):
        return pltpu.make_async_remote_copy(
            src_ref=src, dst_ref=dst, send_sem=send.at[d], recv_sem=recv.at[d],
            device_id=(row_peer(d), my_c), device_id_type=MESH)

    def to_col(src, dst, send, recv, d, peer):
        return pltpu.make_async_remote_copy(
            src_ref=src, dst_ref=dst, send_sem=send.at[d], recv_sem=recv.at[d],
            device_id=(my_r, peer), device_id_type=MESH)

    def fetch(q):
        return pltpu.make_async_copy(
            values_ref.at[pl.ds(q * per, per)], vals.at[pl.ds(q * per, per)], val_sem.at[q])

    bring = [
        pltpu.make_async_copy(src, dst, in_sem.at[i])
        for i, (src, dst) in enumerate((
            (rows_hbm, rows_ref), (cols_hbm, cols_ref), (feat_ref, feat_all.at[my_r]),
            (weight_hbm, weight_ref), (bias_hbm, bias_ref), (gout_hbm, gout_ref)))
    ]
    bring[0].start()
    bring[1].start()
    for q in range(CHUNKS):
        fetch(q).start()
    for copy in bring[2:]:
        copy.start()

    barrier = pltpu.get_barrier_semaphore()
    for d in range(1, n_row):
        pl.semaphore_signal(barrier, inc=1, device_id=(row_peer(d), my_c), device_id_type=MESH)
    for d in range(1, n_col):
        pl.semaphore_signal(barrier, inc=1, device_id=(my_r, col_peer(d)), device_id_type=MESH)

    tiles = row_tiles * col_tiles
    lane = lax.broadcasted_iota(jnp.int32, (slots, slots), 1)
    sub = lax.broadcasted_iota(jnp.int32, (slots, slots), 0)
    live = lane < count_ref[0, 0]
    bring[0].wait()
    bring[1].wait()
    key = jnp.where(
        live, jnp.broadcast_to(rows_ref[...] * col_tiles + cols_ref[...], (slots, slots)), tiles)
    key_t = key.T
    ahead = (key_t < key) | ((key_t == key) & (sub < lane))
    rank = jnp.sum(ahead.astype(jnp.int32), axis=0, keepdims=True)
    hit = jnp.broadcast_to(rank, (slots, slots)).T == lane
    idx_v[0:1, :] = jnp.sum(jnp.where(hit, sub, 0), axis=0, keepdims=True)
    idx_v[1:2, :] = jnp.sum(jnp.where(hit, key_t, 0), axis=0, keepdims=True)
    for q in range(-(-tiles // slots)):
        upto = (key_t <= lane + q * slots).astype(jnp.int32)
        idx_v[2 + q : 3 + q, :] = jnp.sum(upto, axis=0, keepdims=True)
    idx_copy = pltpu.make_async_copy(idx_v, idx_s, idx_sem)
    idx_copy.start()

    pl.semaphore_wait(barrier, n_row + n_col - 2)

    def feat_copy(d):
        return to_row(feat_ref, feat_all.at[my_r], f_send, f_recv, d)

    for d in range(1, n_row):
        feat_copy(d).start()

    idx_copy.wait()
    for q in range(CHUNKS):
        fetch(q).wait()

    def add_slot(i, acc):
        same = (i > 0) & (idx_s[1, i] == idx_s[1, jnp.maximum(i - 1, 0)])
        keep = jnp.where(same, 1.0, 0.0).astype(F32)
        acc = acc * keep + vals[idx_s[0, i]].astype(F32)
        seq[i] = acc.astype(BF16)
        return acc

    lax.fori_loop(0, slots, add_slot, jnp.zeros((side, side), F32), unroll=8)

    def dense_tile(r, c):
        k = r * col_tiles + c
        before = jnp.maximum(k - 1, 0)
        end = idx_s[2 + k // slots, lax.rem(k, slots)]
        start = jnp.where(k > 0, idx_s[2 + before // slots, lax.rem(before, slots)], 0)
        some = jnp.where(end > start, 1.0, 0.0).astype(F32)
        return (seq[jnp.maximum(end - 1, 0)].astype(F32) * some).astype(BF16)

    tiles_per = share // side

    def place(r, _):
        block, inner = r // tiles_per, lax.rem(r, tiles_per)
        at = (lax.rem(block, 2) * n_chip + block // 2) * tiles_per + inner
        for c in range(col_tiles):
            dense[pl.ds(pl.multiple_of(at * side, side), side), c * side : (c + 1) * side] = (
                dense_tile(r, c))
        return 0

    lax.fori_loop(0, row_tiles, place, 0)

    for copy in bring[2:]:
        copy.wait()
    for d in range(1, n_row):
        feat_copy(d).wait_recv()

    def aggregate(block):
        return jnp.dot(
            dense[pl.ds(pl.multiple_of(block * share, share), share), :],
            feat_all[...].reshape(n_row * share, width), preferred_element_type=F32)

    def pair_copy(d):
        return to_col(pair_send.at[d], pair_recv.at[d], p_send, p_recv, d, sibling)

    def part_copy(d):
        return to_col(part_send.at[d], part_recv.at[d], q_send, q_recv, d, chip_peer(d))

    def pair_step(i):
        d = lax.rem(i + 1, n_chip)
        pair_send[d] = aggregate((1 - core) * n_chip + lax.rem(chip + d, n_chip)).astype(BF16)
        pair_copy(d).start()

    def part_step(i):
        d = i + 1
        mine = aggregate(core * n_chip + lax.rem(chip + d, n_chip))
        pair_copy(d).wait_recv()
        part_send[d] = (mine + pair_recv[d].astype(F32)).astype(BF16)
        part_copy(d).start()

    each(n_chip, pair_step)
    each(n_chip - 1, part_step)
    gathered = aggregate(core * n_chip + chip)
    pair_copy(0).wait_recv()
    gathered = gathered + pair_recv[0].astype(F32)

    def turn(r, _):
        for c in range(col_tiles):
            tile = dense[pl.ds(pl.multiple_of(r * side, side), side), c * side : (c + 1) * side]
            dense_t[c * side : (c + 1) * side, pl.ds(pl.multiple_of(r * side, side), side)] = (
                tile.astype(F32).T.astype(BF16))
        return 0

    lax.fori_loop(0, row_tiles, turn, 0)

    for d in range(1, n_chip):
        part_copy(d).wait_recv()
        gathered = gathered + part_recv[d].astype(F32)

    pre = jnp.dot(
        gathered.astype(BF16), weight_ref[...], preferred_element_type=F32) + bias_ref[...]
    low = jnp.exp(jnp.minimum(pre, 0.0))
    grad = (gout_ref[...].astype(F32) * jnp.where(pre > 0, 1.0, low)).astype(BF16)

    def rows_of(block):
        return grad_all.at[pl.ds(pl.multiple_of(block * share, share), share), :]

    mine_at = core * n_chip + chip
    grad_all[pl.ds(pl.multiple_of(mine_at * share, share), share), :] = grad

    def grad_copy(d):
        return to_col(rows_of(mine_at), rows_of(mine_at), g_send, g_recv, d, chip_peer(d))

    def hand_copy(d):
        at = core * n_chip + lax.rem(chip + n_chip - d, n_chip)
        return to_col(rows_of(at), rows_of(at), h_send, h_recv, d, sibling)

    for d in range(1, n_chip):
        grad_copy(d).start()
    hand_copy(0).start()
    out_ref[...] = jnp.where(pre > 0, pre, low - 1.0).astype(BF16)
    out_copy = pltpu.make_async_copy(out_ref, out_hbm, out_sem.at[0])
    out_copy.start()

    def gw_copy(d):
        return to_col(gw_send.at[col_peer(d)], gw_recv.at[d], w_send, w_recv, d, col_peer(d))

    term = jnp.dot(gathered.T.astype(BF16), grad, preferred_element_type=F32)
    gw_send[...] = term.astype(gw_send.dtype).reshape(n_col, chunk, width)
    for d in range(1, n_col):
        gw_copy(d).start()

    for d in range(1, n_chip):
        grad_copy(d).wait_recv()
        hand_copy(d).start()
    for d in range(n_chip):
        hand_copy(d).wait_recv()

    def back_copy(d):
        return to_row(back_send.at[d], back_recv.at[d], b_send, b_recv, d)

    def backward(i):
        return jnp.dot(
            dense_t[pl.ds(pl.multiple_of(i * share, share), share), :], grad_all[...],
            preferred_element_type=F32)

    def backward_send(i):
        d = i + 1
        back_send[d] = backward(row_peer(d)).astype(BF16)
        back_copy(d).start()

    each(n_row - 1, backward_send)

    gw_sum = gw_send[my_c].astype(F32)
    for d in range(1, n_col):
        gw_copy(d).wait_recv()
        gw_sum = gw_sum + gw_recv[d].astype(F32)

    def gwz_copy(d):
        return to_row(gwz_recv.at[my_r], gwz_recv.at[my_r], z_send, z_recv, d)

    gwz_recv[my_r] = gw_sum.astype(gw_send.dtype)
    for d in range(1, n_row):
        gwz_copy(d).start()

    def gb_copy(d):
        return to_row(gb_recv.at[my_r], gb_recv.at[my_r], s_send, s_recv, d)

    ones = jnp.ones((16, n_col * share), BF16)
    gb_recv[my_r] = jnp.dot(ones, grad_all[...], preferred_element_type=F32)[:8]
    for d in range(1, n_row):
        gb_copy(d).start()

    total = backward(my_r)

    for d in range(1, n_row):
        gwz_copy(d).wait_recv()
    whole = gwz_recv[0].astype(F32)
    for i in range(1, n_row):
        whole = whole + gwz_recv[i].astype(F32)

    def all_copy(d):
        return to_col(gw_all.at[my_c], gw_all.at[my_c], a_send, a_recv, d, col_peer(d))

    gw_all[my_c] = whole.astype(gw_all.dtype)
    for d in range(1, n_col):
        all_copy(d).start()

    for d in range(1, n_row):
        back_copy(d).wait_recv()
        total = total + back_recv[d].astype(F32)
    gmix_ref[...] = total.astype(BF16)

    for d in range(1, n_row):
        gb_copy(d).wait_recv()
    gb_copy_out = pltpu.make_async_copy(gb_recv, gb_hbm, out_sem.at[1])
    gb_copy_out.start()

    for d in range(1, n_row):
        feat_copy(d).wait_send()
        back_copy(d).wait_send()
        gwz_copy(d).wait_send()
        gb_copy(d).wait_send()
    for d in range(n_chip):
        pair_copy(d).wait_send()
        hand_copy(d).wait_send()
    for d in range(1, n_chip):
        part_copy(d).wait_send()
        grad_copy(d).wait_send()
    for d in range(1, n_col):
        all_copy(d).wait_recv()
    gw_copy_out = pltpu.make_async_copy(gw_all, gw_hbm, out_sem.at[2])
    gw_copy_out.start()
    for d in range(1, n_col):
        gw_copy(d).wait_send()
        all_copy(d).wait_send()
    out_copy.wait()
    gb_copy_out.wait()
    gw_copy_out.wait()


def finish(part_ref, gmix_ref, gwp_ref, gbp_ref, weight_ref, out_ref, gfeat_ref, gw_ref, gb_ref):
    out_ref[...] = part_ref[...]
    gfeat_ref[...] = lax.dot_general(
        gmix_ref[...], weight_ref[...], (((1,), (1,)), ((), ())),
        preferred_element_type=F32).astype(BF16)
    gw_ref[...] = gwp_ref[...].astype(F32).reshape(gw_ref.shape)
    gb = gbp_ref[0]
    for i in range(1, gbp_ref.shape[0]):
        gb = gb + gbp_ref[i]
    gb_ref[...] = gb[0:1]


def body(n_row, n_col, features, weight, bias, grad_out, tile_rows, tile_cols, tile_counts, tile_values):
    values = tile_values[0, 0]
    slots, side = values.shape[0], values.shape[1]
    share, width = features.shape
    row_tiles = share * n_col // side
    col_tiles = share * n_row // side
    chunk = width // n_col
    gw_type = BF16 if chunk % 16 == 0 else F32
    index_rows = -(-(2 + -(-(row_tiles * col_tiles) // slots)) // 8) * 8
    vmem = pl.BlockSpec(memory_space=pltpu.VMEM)
    smem = pl.BlockSpec(memory_space=pltpu.SMEM)
    anywhere = pl.BlockSpec(memory_space=pl.ANY)
    dma = pltpu.SemaphoreType.DMA
    row_sem, col_sem, chip_sem = dma((n_row,)), dma((n_col,)), dma((n_col // 2,))
    buffers = [
        ((width, width), BF16),
        ((1, width), F32),
        ((share, width), BF16),
        ((1, slots), jnp.int32),
        ((1, slots), jnp.int32),
        ((share, width), BF16),
        ((slots, side, side), BF16),
        ((slots, side, side), BF16),
        ((row_tiles * side, col_tiles * side), BF16),
        ((col_tiles * side, row_tiles * side), BF16),
        ((n_row, share, width), BF16),
        ((n_col // 2, share, width), BF16),
        ((n_col // 2, share, width), BF16),
        ((n_col // 2, share, width), BF16),
        ((n_col // 2, share, width), BF16),
        ((n_col * share, width), BF16),
        ((n_row, share, width), BF16),
        ((n_row, share, width), BF16),
        ((n_col, chunk, width), gw_type),
        ((n_col, chunk, width), gw_type),
        ((n_row, chunk, width), gw_type),
        ((n_col, chunk, width), gw_type),
        ((n_row, 8, width), F32),
        ((index_rows, slots), jnp.int32),
    ]
    out, gmix, gw, gb = pl.pallas_call(
        functools.partial(kernel, n_row, n_col, row_tiles, col_tiles),
        out_shape=(
            jax.ShapeDtypeStruct((share, width), BF16),
            jax.ShapeDtypeStruct((share, width), BF16),
            jax.ShapeDtypeStruct((n_col, chunk, width), gw_type),
            jax.ShapeDtypeStruct((n_row, 8, width), F32),
        ),
        in_specs=[anywhere] * 6 + [smem, anywhere],
        out_specs=(anywhere, vmem, anywhere, anywhere),
        scratch_shapes=[pltpu.VMEM(shape, kind) for shape, kind in buffers] + [
            pltpu.SMEM((index_rows, slots), jnp.int32),
            dma((CHUNKS,)), dma(()), dma((6,)), dma((3,)),
            row_sem, row_sem, chip_sem, chip_sem, chip_sem, chip_sem, chip_sem, chip_sem,
            chip_sem, chip_sem, row_sem, row_sem,
            col_sem, col_sem, row_sem, row_sem, col_sem, col_sem, row_sem, row_sem,
        ],
        compiler_params=pltpu.CompilerParams(
            collective_id=0, has_side_effects=True,
            vmem_limit_bytes=VMEM_BYTES),
        cost_estimate=pl.CostEstimate(
            flops=4 * row_tiles * col_tiles * side * side * width,
            bytes_accessed=2 * slots * side * side, transcendentals=share * width),
    )(features, weight, bias[None, :], grad_out, tile_rows[0], tile_cols[0], tile_counts, values)
    out, gfeat, gw, gb = pl.pallas_call(
        finish,
        out_shape=(
            jax.ShapeDtypeStruct((share, width), BF16),
            jax.ShapeDtypeStruct((share, width), BF16),
            jax.ShapeDtypeStruct((width, width), F32),
            jax.ShapeDtypeStruct((1, width), F32),
        ),
        in_specs=[vmem] * 5,
        out_specs=(vmem, vmem, vmem, vmem),
        compiler_params=pltpu.CompilerParams(vmem_limit_bytes=VMEM_BYTES),
    )(out, gmix, gw, gb, weight)
    return out, gfeat, gw, gb[0]


def solution(mesh):
    placed = (
        P(("col", "row"), None),
        P(),
        P(),
        P(("row", "col"), None),
        P("row", "col", None),
        P("row", "col", None),
        P("row", "col"),
        P("row", "col", None, None, None),
    )
    return jax.shard_map(
        functools.partial(body, mesh.shape["row"], mesh.shape["col"]),
        mesh=mesh,
        in_specs=placed,
        out_specs=(P(("row", "col"), None), P(("col", "row"), None), P(), P()),
        check_vma=False,
    )
```

```python
import functools

import jax
import jax.numpy as jnp
from jax import lax
from jax.experimental import pallas as pl
from jax.experimental.pallas import tpu as pltpu
from jax.sharding import PartitionSpec as P

MESH = pl.DeviceIdType.MESH
CHUNKS = 4
VMEM_BYTES = 60 * 2**20
F32 = jnp.float32
BF16 = jnp.bfloat16


def each(n, step):
    if n <= 8:
        for i in range(n):
            step(i)
    else:
        lax.fori_loop(0, n, lambda i, _: (step(i), 0)[1], 0)


def kernel(
    n_row, n_col, row_tiles, col_tiles,
    feat_ref, weight_hbm, bias_hbm, gout_hbm, rows_hbm, cols_hbm, count_ref, values_ref,
    out_hbm, gmix_ref, gw_hbm, gb_hbm,
    weight_ref, bias_ref, gout_ref, rows_ref, cols_ref, out_ref,
    vals, seq, dense, dense_t, feat_all, pair_send, pair_recv, part_send, part_recv, grad_all,
    own_sum, back_sum,
    back_send, back_recv, gw_send, gw_recv, gwz_recv, gw_all, gb_recv, idx_v, idx_s,
    val_sem, idx_sem, in_sem, out_sem, f_send, f_recv, p_send, p_recv, q_send, q_recv, g_send, g_recv,
    h_send, h_recv, b_send, b_recv,
    w_send, w_recv, z_send, z_recv, a_send, a_recv, s_send, s_recv,
):
    my_r = lax.axis_index("row")
    my_c = lax.axis_index("col")
    n_chip = n_col // 2
    core, chip = lax.rem(my_c, 2), my_c // 2
    sibling = my_c + 1 - 2 * core
    slots, side = vals.shape[0], vals.shape[1]
    share, width = feat_ref.shape
    per = slots // CHUNKS
    chunk = width // n_col

    def row_peer(d):
        return lax.rem(my_r + d, n_row)

    def col_peer(d):
        return lax.rem(my_c + d, n_col)

    def chip_peer(d):
        return 2 * lax.rem(chip + d, n_chip) + core

    def to_row(src, dst, send, recv, d):
        return pltpu.make_async_remote_copy(
            src_ref=src, dst_ref=dst, send_sem=send.at[d], recv_sem=recv.at[d],
            device_id=(row_peer(d), my_c), device_id_type=MESH)

    def to_col(src, dst, send, recv, d, peer):
        return pltpu.make_async_remote_copy(
            src_ref=src, dst_ref=dst, send_sem=send.at[d], recv_sem=recv.at[d],
            device_id=(my_r, peer), device_id_type=MESH)

    def fetch(q):
        return pltpu.make_async_copy(
            values_ref.at[pl.ds(q * per, per)], vals.at[pl.ds(q * per, per)], val_sem.at[q])

    bring = [
        pltpu.make_async_copy(src, dst, in_sem.at[i])
        for i, (src, dst) in enumerate((
            (rows_hbm, rows_ref), (cols_hbm, cols_ref), (feat_ref, feat_all.at[my_r]),
            (weight_hbm, weight_ref), (bias_hbm, bias_ref), (gout_hbm, gout_ref)))
    ]
    bring[0].start()
    bring[1].start()
    for q in range(CHUNKS):
        fetch(q).start()
    for copy in bring[2:]:
        copy.start()

    barrier = pltpu.get_barrier_semaphore()
    for d in range(1, n_row):
        pl.semaphore_signal(barrier, inc=1, device_id=(row_peer(d), my_c), device_id_type=MESH)
    for d in range(1, n_col):
        pl.semaphore_signal(barrier, inc=1, device_id=(my_r, col_peer(d)), device_id_type=MESH)

    pl.semaphore_wait(barrier, n_row + n_col - 2)

    def feat_copy(d):
        return to_row(feat_ref, feat_all.at[my_r], f_send, f_recv, d)

    for d in range(1, n_row):
        feat_copy(d).start()

    tiles = row_tiles * col_tiles
    lane = lax.broadcasted_iota(jnp.int32, (slots, slots), 1)
    sub = lax.broadcasted_iota(jnp.int32, (slots, slots), 0)
    live = lane < count_ref[0, 0]
    bring[0].wait()
    bring[1].wait()
    key = jnp.where(
        live, jnp.broadcast_to(rows_ref[...] * col_tiles + cols_ref[...], (slots, slots)), tiles)
    key_t = key.T
    ahead = (key_t < key) | ((key_t == key) & (sub < lane))
    rank = jnp.sum(ahead.astype(jnp.int32), axis=0, keepdims=True)
    hit = jnp.broadcast_to(rank, (slots, slots)).T == lane
    idx_v[0:1, :] = jnp.sum(jnp.where(hit, sub, 0), axis=0, keepdims=True)
    idx_v[1:2, :] = jnp.sum(jnp.where(hit, key_t, 0), axis=0, keepdims=True)
    for q in range(-(-tiles // slots)):
        upto = (key_t <= lane + q * slots).astype(jnp.int32)
        idx_v[2 + q : 3 + q, :] = jnp.sum(upto, axis=0, keepdims=True)
    idx_copy = pltpu.make_async_copy(idx_v, idx_s, idx_sem)
    idx_copy.start()


    idx_copy.wait()
    for q in range(CHUNKS):
        fetch(q).wait()

    def add_slot(i, acc):
        same = (i > 0) & (idx_s[1, i] == idx_s[1, jnp.maximum(i - 1, 0)])
        keep = jnp.where(same, 1.0, 0.0).astype(F32)
        acc = acc * keep + vals[idx_s[0, i]].astype(F32)
        seq[i] = acc.astype(BF16)
        return acc

    lax.fori_loop(0, slots, add_slot, jnp.zeros((side, side), F32), unroll=8)

    def dense_tile(r, c):
        k = r * col_tiles + c
        before = jnp.maximum(k - 1, 0)
        end = idx_s[2 + k // slots, lax.rem(k, slots)]
        start = jnp.where(k > 0, idx_s[2 + before // slots, lax.rem(before, slots)], 0)
        some = jnp.where(end > start, 1.0, 0.0).astype(F32)
        return (seq[jnp.maximum(end - 1, 0)].astype(F32) * some).astype(BF16)

    tiles_per = share // side

    def place(r, _):
        block, inner = r // tiles_per, lax.rem(r, tiles_per)
        at = (lax.rem(block, 2) * n_chip + block // 2) * tiles_per + inner
        for c in range(col_tiles):
            dense[pl.ds(pl.multiple_of(at * side, side), side), c * side : (c + 1) * side] = (
                dense_tile(r, c))
        return 0

    lax.fori_loop(0, row_tiles, place, 0)

    for copy in bring[2:]:
        copy.wait()
    for d in range(1, n_row):
        feat_copy(d).wait_recv()

    half = n_chip * share

    def group(n, step):
        size = 4 if n % 4 == 0 else 1
        each(n // size, lambda g: step(g * size * share, size * share))

    def rows_at(start, count):
        return pl.ds(pl.multiple_of(start, share), count)

    def aggregate(start, count):
        return jnp.dot(
            dense[rows_at(start, count), :], feat_all[...].reshape(n_row * share, width),
            preferred_element_type=F32)

    def chip_rows(d):
        return rows_at(lax.rem(chip + d, n_chip) * share, share)

    def pair_copy(d):
        return to_col(
            pair_send.at[chip_rows(d), :], pair_recv.at[d], p_send, p_recv, d, sibling)

    def part_copy(d):
        return to_col(part_send.at[d], part_recv.at[d], q_send, q_recv, d, chip_peer(d))

    def pair_step(start, count):
        pair_send[rows_at(start, count), :] = (
            aggregate((1 - core) * half + start, count).astype(BF16))

    def own_step(start, count):
        own_sum[rows_at(start, count), :] = aggregate(core * half + start, count)

    group(n_chip, pair_step)
    for d in range(n_chip):
        pair_copy((d + 1) % n_chip).start()
    group(n_chip, own_step)
    for d in range(1, n_chip):
        pair_copy(d).wait_recv()
        part_send[d] = (own_sum[chip_rows(d), :] + pair_recv[d].astype(F32)).astype(BF16)
        part_copy(d).start()
    pair_copy(0).wait_recv()
    gathered = own_sum[chip_rows(0), :] + pair_recv[0].astype(F32)

    def turn(r, _):
        for c in range(col_tiles):
            tile = dense[pl.ds(pl.multiple_of(r * side, side), side), c * side : (c + 1) * side]
            dense_t[c * side : (c + 1) * side, pl.ds(pl.multiple_of(r * side, side), side)] = (
                tile.astype(F32).T.astype(BF16))
        return 0

    lax.fori_loop(0, row_tiles, turn, 0)

    for d in range(1, n_chip):
        part_copy(d).wait_recv()
        gathered = gathered + part_recv[d].astype(F32)

    pre = jnp.dot(
        gathered.astype(BF16), weight_ref[...], preferred_element_type=F32) + bias_ref[...]
    low = jnp.exp(jnp.minimum(pre, 0.0))
    grad = (gout_ref[...].astype(F32) * jnp.where(pre > 0, 1.0, low)).astype(BF16)

    def rows_of(block):
        return grad_all.at[pl.ds(pl.multiple_of(block * share, share), share), :]

    mine_at = core * n_chip + chip
    grad_all[pl.ds(pl.multiple_of(mine_at * share, share), share), :] = grad

    def grad_copy(d):
        return to_col(rows_of(mine_at), rows_of(mine_at), g_send, g_recv, d, chip_peer(d))

    def hand_copy(d):
        at = core * n_chip + lax.rem(chip + n_chip - d, n_chip)
        return to_col(rows_of(at), rows_of(at), h_send, h_recv, d, sibling)

    for d in range(1, n_chip):
        grad_copy(d).start()
    hand_copy(0).start()
    out_ref[...] = jnp.where(pre > 0, pre, low - 1.0).astype(BF16)
    out_copy = pltpu.make_async_copy(out_ref, out_hbm, out_sem.at[0])
    out_copy.start()

    def gw_copy(d):
        return to_col(gw_send.at[col_peer(d)], gw_recv.at[d], w_send, w_recv, d, col_peer(d))

    term = jnp.dot(gathered.T.astype(BF16), grad, preferred_element_type=F32)
    gw_send[...] = term.astype(gw_send.dtype).reshape(n_col, chunk, width)
    for d in range(1, n_col):
        gw_copy(d).start()

    for d in range(1, n_chip):
        grad_copy(d).wait_recv()
        hand_copy(d).start()
    def back_copy(d):
        return to_row(back_send.at[d], back_recv.at[d], b_send, b_recv, d)

    def half_product(start, count, side_core):
        at = pl.ds(pl.multiple_of(side_core * half, share), half)
        return jnp.dot(
            dense_t[rows_at(start, count), at], grad_all[at, :], preferred_element_type=F32)

    def first_step(start, count):
        back_sum[rows_at(start, count), :] = half_product(start, count, core)

    def backward(i):
        return back_sum[rows_at(i * share, share), :] + half_product(i * share, share, 1 - core)

    group(n_row, first_step)
    for d in range(n_chip):
        hand_copy(d).wait_recv()
    back_send[1] = backward(row_peer(1)).astype(BF16)

    gw_sum = gw_send[my_c].astype(F32)
    for d in range(1, n_col):
        gw_copy(d).wait_recv()
        gw_sum = gw_sum + gw_recv[d].astype(F32)

    def gwz_copy(d):
        return to_row(gwz_recv.at[my_r], gwz_recv.at[my_r], z_send, z_recv, d)

    gwz_recv[my_r] = gw_sum.astype(gw_send.dtype)
    for d in range(1, n_row):
        gwz_copy(d).start()
    back_copy(1).start()

    def backward_send(i):
        d = i + 2
        back_send[d] = backward(row_peer(d)).astype(BF16)
        back_copy(d).start()

    each(n_row - 2, backward_send)

    def gb_copy(d):
        return to_row(gb_recv.at[my_r], gb_recv.at[my_r], s_send, s_recv, d)

    ones = jnp.ones((16, n_col * share), BF16)
    gb_recv[my_r] = jnp.dot(ones, grad_all[...], preferred_element_type=F32)[:8]
    for d in range(1, n_row):
        gb_copy(d).start()

    total = backward(my_r)

    for d in range(1, n_row):
        gwz_copy(d).wait_recv()
    whole = gwz_recv[0].astype(F32)
    for i in range(1, n_row):
        whole = whole + gwz_recv[i].astype(F32)

    def all_copy(d):
        return to_col(gw_all.at[my_c], gw_all.at[my_c], a_send, a_recv, d, col_peer(d))

    gw_all[my_c] = whole.astype(gw_all.dtype)
    for d in range(1, n_col):
        all_copy(d).start()

    for d in range(1, n_row):
        back_copy(d).wait_recv()
        total = total + back_recv[d].astype(F32)
    gmix_ref[...] = total.astype(BF16)

    for d in range(1, n_row):
        gb_copy(d).wait_recv()
    gb_copy_out = pltpu.make_async_copy(gb_recv, gb_hbm, out_sem.at[1])
    gb_copy_out.start()

    for d in range(1, n_row):
        feat_copy(d).wait_send()
        back_copy(d).wait_send()
        gwz_copy(d).wait_send()
        gb_copy(d).wait_send()
    for d in range(n_chip):
        pair_copy(d).wait_send()
        hand_copy(d).wait_send()
    for d in range(1, n_chip):
        part_copy(d).wait_send()
        grad_copy(d).wait_send()
    for d in range(1, n_col):
        all_copy(d).wait_recv()
    gw_copy_out = pltpu.make_async_copy(gw_all, gw_hbm, out_sem.at[2])
    gw_copy_out.start()
    for d in range(1, n_col):
        gw_copy(d).wait_send()
        all_copy(d).wait_send()
    out_copy.wait()
    gb_copy_out.wait()
    gw_copy_out.wait()


def finish(part_ref, gmix_ref, gwp_ref, gbp_ref, weight_ref, out_ref, gfeat_ref, gw_ref, gb_ref):
    out_ref[...] = part_ref[...]
    gfeat_ref[...] = lax.dot_general(
        gmix_ref[...], weight_ref[...], (((1,), (1,)), ((), ())),
        preferred_element_type=F32).astype(BF16)
    gw_ref[...] = gwp_ref[...].astype(F32).reshape(gw_ref.shape)
    gb = gbp_ref[0]
    for i in range(1, gbp_ref.shape[0]):
        gb = gb + gbp_ref[i]
    gb_ref[...] = gb[0:1]


def body(n_row, n_col, features, weight, bias, grad_out, tile_rows, tile_cols, tile_counts, tile_values):
    values = tile_values[0, 0]
    slots, side = values.shape[0], values.shape[1]
    share, width = features.shape
    row_tiles = share * n_col // side
    col_tiles = share * n_row // side
    chunk = width // n_col
    gw_type = BF16 if chunk % 16 == 0 else F32
    index_rows = -(-(2 + -(-(row_tiles * col_tiles) // slots)) // 8) * 8
    vmem = pl.BlockSpec(memory_space=pltpu.VMEM)
    smem = pl.BlockSpec(memory_space=pltpu.SMEM)
    anywhere = pl.BlockSpec(memory_space=pl.ANY)
    dma = pltpu.SemaphoreType.DMA
    row_sem, col_sem, chip_sem = dma((n_row,)), dma((n_col,)), dma((n_col // 2,))
    buffers = [
        ((width, width), BF16),
        ((1, width), F32),
        ((share, width), BF16),
        ((1, slots), jnp.int32),
        ((1, slots), jnp.int32),
        ((share, width), BF16),
        ((slots, side, side), BF16),
        ((slots, side, side), BF16),
        ((row_tiles * side, col_tiles * side), BF16),
        ((col_tiles * side, row_tiles * side), BF16),
        ((n_row, share, width), BF16),
        ((n_col // 2 * share, width), BF16),
        ((n_col // 2, share, width), BF16),
        ((n_col // 2, share, width), BF16),
        ((n_col // 2, share, width), BF16),
        ((n_col * share, width), BF16),
        ((n_col // 2 * share, width), F32),
        ((n_row * share, width), F32),
        ((n_row, share, width), BF16),
        ((n_row, share, width), BF16),
        ((n_col, chunk, width), gw_type),
        ((n_col, chunk, width), gw_type),
        ((n_row, chunk, width), gw_type),
        ((n_col, chunk, width), gw_type),
        ((n_row, 8, width), F32),
        ((index_rows, slots), jnp.int32),
    ]
    out, gmix, gw, gb = pl.pallas_call(
        functools.partial(kernel, n_row, n_col, row_tiles, col_tiles),
        out_shape=(
            jax.ShapeDtypeStruct((share, width), BF16),
            jax.ShapeDtypeStruct((share, width), BF16),
            jax.ShapeDtypeStruct((n_col, chunk, width), gw_type),
            jax.ShapeDtypeStruct((n_row, 8, width), F32),
        ),
        in_specs=[anywhere] * 6 + [smem, anywhere],
        out_specs=(anywhere, vmem, anywhere, anywhere),
        scratch_shapes=[pltpu.VMEM(shape, kind) for shape, kind in buffers] + [
            pltpu.SMEM((index_rows, slots), jnp.int32),
            dma((CHUNKS,)), dma(()), dma((6,)), dma((3,)),
            row_sem, row_sem, chip_sem, chip_sem, chip_sem, chip_sem, chip_sem, chip_sem,
            chip_sem, chip_sem, row_sem, row_sem,
            col_sem, col_sem, row_sem, row_sem, col_sem, col_sem, row_sem, row_sem,
        ],
        compiler_params=pltpu.CompilerParams(
            collective_id=0, has_side_effects=True,
            vmem_limit_bytes=VMEM_BYTES),
        cost_estimate=pl.CostEstimate(
            flops=4 * row_tiles * col_tiles * side * side * width,
            bytes_accessed=2 * slots * side * side, transcendentals=share * width),
    )(features, weight, bias[None, :], grad_out, tile_rows[0], tile_cols[0], tile_counts, values)
    out, gfeat, gw, gb = pl.pallas_call(
        finish,
        out_shape=(
            jax.ShapeDtypeStruct((share, width), BF16),
            jax.ShapeDtypeStruct((share, width), BF16),
            jax.ShapeDtypeStruct((width, width), F32),
            jax.ShapeDtypeStruct((1, width), F32),
        ),
        in_specs=[vmem] * 5,
        out_specs=(vmem, vmem, vmem, vmem),
        compiler_params=pltpu.CompilerParams(vmem_limit_bytes=VMEM_BYTES),
    )(out, gmix, gw, gb, weight)
    return out, gfeat, gw, gb[0]


def solution(mesh):
    placed = (
        P(("col", "row"), None),
        P(),
        P(),
        P(("row", "col"), None),
        P("row", "col", None),
        P("row", "col", None),
        P("row", "col"),
        P("row", "col", None, None, None),
    )
    return jax.shard_map(
        functools.partial(body, mesh.shape["row"], mesh.shape["col"]),
        mesh=mesh,
        in_specs=placed,
        out_specs=(P(("row", "col"), None), P(("col", "row"), None), P(), P()),
        check_vma=False,
    )
```

```python
import functools

import jax
import jax.numpy as jnp
from jax import lax
from jax.experimental import pallas as pl
from jax.experimental.pallas import tpu as pltpu
from jax.sharding import PartitionSpec as P

MESH = pl.DeviceIdType.MESH
CHUNKS = 4
PARTS = 2
VMEM_BYTES = 60 * 2**20
F32 = jnp.float32
BF16 = jnp.bfloat16


def each(n, step):
    if n <= 8:
        for i in range(n):
            step(i)
    else:
        lax.fori_loop(0, n, lambda i, _: (step(i), 0)[1], 0)


def kernel(
    n_row, n_col, row_tiles, col_tiles,
    feat_ref, weight_hbm, bias_hbm, gout_hbm, rows_hbm, cols_hbm, count_ref, values_ref,
    out_hbm, gmix_ref, gw_hbm, gb_hbm,
    weight_ref, bias_ref, gout_ref, rows_ref, cols_ref, out_ref,
    vals, seq, dense, dense_t, feat_all, pair_send, pair_recv, part_send, part_recv, grad_all,
    own_sum, back_sum,
    back_send, back_recv, gw_send, gw_recv, gwz_recv, gw_all, gb_recv, idx_v, idx_s,
    val_sem, idx_sem, in_sem, out_sem, f_send, f_recv, p_send, p_recv, q_send, q_recv, g_send, g_recv,
    h_send, h_recv, b_send, b_recv,
    w_send, w_recv, z_send, z_recv, a_send, a_recv, s_send, s_recv,
):
    my_r = lax.axis_index("row")
    my_c = lax.axis_index("col")
    n_chip = n_col // 2
    core, chip = lax.rem(my_c, 2), my_c // 2
    sibling = my_c + 1 - 2 * core
    slots, side = vals.shape[0], vals.shape[1]
    share, width = feat_ref.shape
    per = slots // CHUNKS
    chunk = width // n_col
    part = width // PARTS

    def lanes(h):
        return slice(h * part, (h + 1) * part)

    def row_peer(d):
        return lax.rem(my_r + d, n_row)

    def col_peer(d):
        return lax.rem(my_c + d, n_col)

    def chip_peer(d):
        return 2 * lax.rem(chip + d, n_chip) + core

    def to_row(src, dst, send, recv, d, h=0):
        return pltpu.make_async_remote_copy(
            src_ref=src, dst_ref=dst, send_sem=send.at[h * n_row + d], recv_sem=recv.at[h * n_row + d],
            device_id=(row_peer(d), my_c), device_id_type=MESH)

    def to_col(src, dst, send, recv, d, peer, h=0):
        return pltpu.make_async_remote_copy(
            src_ref=src, dst_ref=dst, send_sem=send.at[h * n_chip + d], recv_sem=recv.at[h * n_chip + d],
            device_id=(my_r, peer), device_id_type=MESH)

    def fetch(q):
        return pltpu.make_async_copy(
            values_ref.at[pl.ds(q * per, per)], vals.at[pl.ds(q * per, per)], val_sem.at[q])

    bring = [
        pltpu.make_async_copy(src, dst, in_sem.at[i])
        for i, (src, dst) in enumerate((
            (rows_hbm, rows_ref), (cols_hbm, cols_ref), (weight_hbm, weight_ref),
            (bias_hbm, bias_ref), (gout_hbm, gout_ref),
            *((feat_ref.at[:, lanes(h)], feat_all.at[h, my_r]) for h in range(PARTS))))
    ]
    bring[0].start()
    bring[1].start()
    for q in range(CHUNKS):
        fetch(q).start()
    for copy in bring[2:]:
        copy.start()

    barrier = pltpu.get_barrier_semaphore()
    for d in range(1, n_row):
        pl.semaphore_signal(barrier, inc=1, device_id=(row_peer(d), my_c), device_id_type=MESH)
    for d in range(1, n_col):
        pl.semaphore_signal(barrier, inc=1, device_id=(my_r, col_peer(d)), device_id_type=MESH)

    pl.semaphore_wait(barrier, n_row + n_col - 2)

    def feat_copy(d, h):
        return to_row(feat_ref.at[:, lanes(h)], feat_all.at[h, my_r], f_send, f_recv, d, h)

    for h in range(PARTS):
        for d in range(1, n_row):
            feat_copy(d, h).start()

    tiles = row_tiles * col_tiles
    lane = lax.broadcasted_iota(jnp.int32, (slots, slots), 1)
    sub = lax.broadcasted_iota(jnp.int32, (slots, slots), 0)
    live = lane < count_ref[0, 0]
    bring[0].wait()
    bring[1].wait()
    key = jnp.where(
        live, jnp.broadcast_to(rows_ref[...] * col_tiles + cols_ref[...], (slots, slots)), tiles)
    key_t = key.T
    ahead = (key_t < key) | ((key_t == key) & (sub < lane))
    rank = jnp.sum(ahead.astype(jnp.int32), axis=0, keepdims=True)
    hit = jnp.broadcast_to(rank, (slots, slots)).T == lane
    idx_v[0:1, :] = jnp.sum(jnp.where(hit, sub, 0), axis=0, keepdims=True)
    idx_v[1:2, :] = jnp.sum(jnp.where(hit, key_t, 0), axis=0, keepdims=True)
    for q in range(-(-tiles // slots)):
        upto = (key_t <= lane + q * slots).astype(jnp.int32)
        idx_v[2 + q : 3 + q, :] = jnp.sum(upto, axis=0, keepdims=True)
    idx_copy = pltpu.make_async_copy(idx_v, idx_s, idx_sem)
    idx_copy.start()


    idx_copy.wait()
    for q in range(CHUNKS):
        fetch(q).wait()

    def add_slot(i, acc):
        same = (i > 0) & (idx_s[1, i] == idx_s[1, jnp.maximum(i - 1, 0)])
        keep = jnp.where(same, 1.0, 0.0).astype(F32)
        acc = acc * keep + vals[idx_s[0, i]].astype(F32)
        seq[i] = acc.astype(BF16)
        return acc

    lax.fori_loop(0, slots, add_slot, jnp.zeros((side, side), F32), unroll=8)

    def dense_tile(r, c):
        k = r * col_tiles + c
        before = jnp.maximum(k - 1, 0)
        end = idx_s[2 + k // slots, lax.rem(k, slots)]
        start = jnp.where(k > 0, idx_s[2 + before // slots, lax.rem(before, slots)], 0)
        some = jnp.where(end > start, 1.0, 0.0).astype(F32)
        return (seq[jnp.maximum(end - 1, 0)].astype(F32) * some).astype(BF16)

    tiles_per = share // side

    def place(r, _):
        block, inner = r // tiles_per, lax.rem(r, tiles_per)
        at = (lax.rem(block, 2) * n_chip + block // 2) * tiles_per + inner
        for c in range(col_tiles):
            dense[pl.ds(pl.multiple_of(at * side, side), side), c * side : (c + 1) * side] = (
                dense_tile(r, c))
        return 0

    lax.fori_loop(0, row_tiles, place, 0)

    for copy in bring[2:]:
        copy.wait()
    half = n_chip * share

    def group(n, step):
        size = 4 if n % 4 == 0 else 1
        each(n // size, lambda g: step(g * size * share, size * share))

    def rows_at(start, count):
        return pl.ds(pl.multiple_of(start, share), count)

    def aggregate(start, count, h):
        return jnp.dot(
            dense[rows_at(start, count), :], feat_all[h].reshape(n_row * share, part),
            preferred_element_type=F32)

    def chip_rows(d):
        return rows_at(lax.rem(chip + d, n_chip) * share, share)

    def pair_copy(d, h):
        return to_col(
            pair_send.at[h, chip_rows(d), :], pair_recv.at[h, d], p_send, p_recv, d, sibling, h)

    def part_copy(d, h):
        return to_col(
            part_send.at[h, d], part_recv.at[h, d], q_send, q_recv, d, chip_peer(d), h)

    for h in range(PARTS):
        def pair_step(start, count):
            pair_send[h, rows_at(start, count), :] = (
                aggregate((1 - core) * half + start, count, h).astype(BF16))

        def own_step(start, count):
            own_sum[h, rows_at(start, count), :] = aggregate(core * half + start, count, h)

        for d in range(1, n_row):
            feat_copy(d, h).wait_recv()
        group(n_chip, pair_step)
        for d in range(n_chip):
            pair_copy((d + 1) % n_chip, h).start()
        group(n_chip, own_step)
        for d in range(1, n_chip):
            pair_copy(d, h).wait_recv()
            part_send[h, d] = (
                own_sum[h, chip_rows(d), :] + pair_recv[h, d].astype(F32)).astype(BF16)
            part_copy(d, h).start()
        pair_copy(0, h).wait_recv()

    def turn(r, _):
        for c in range(col_tiles):
            tile = dense[pl.ds(pl.multiple_of(r * side, side), side), c * side : (c + 1) * side]
            dense_t[c * side : (c + 1) * side, pl.ds(pl.multiple_of(r * side, side), side)] = (
                tile.astype(F32).T.astype(BF16))
        return 0

    lax.fori_loop(0, row_tiles, turn, 0)

    sums = []
    for h in range(PARTS):
        total = own_sum[h, chip_rows(0), :] + pair_recv[h, 0].astype(F32)
        for d in range(1, n_chip):
            part_copy(d, h).wait_recv()
            total = total + part_recv[h, d].astype(F32)
        sums.append(total)
    gathered = jnp.concatenate(sums, axis=1)

    pre = jnp.dot(
        gathered.astype(BF16), weight_ref[...], preferred_element_type=F32) + bias_ref[...]
    low = jnp.exp(jnp.minimum(pre, 0.0))
    grad = (gout_ref[...].astype(F32) * jnp.where(pre > 0, 1.0, low)).astype(BF16)

    def rows_of(block, h):
        return grad_all.at[h, rows_at(block * share, share), :]

    mine_at = core * n_chip + chip
    for h in range(PARTS):
        grad_all[h, rows_at(mine_at * share, share), :] = grad[:, lanes(h)]

    def grad_copy(d, h):
        return to_col(
            rows_of(mine_at, h), rows_of(mine_at, h), g_send, g_recv, d, chip_peer(d), h)

    def hand_copy(d, h):
        at = core * n_chip + lax.rem(chip + n_chip - d, n_chip)
        return to_col(rows_of(at, h), rows_of(at, h), h_send, h_recv, d, sibling, h)

    for h in range(PARTS):
        for d in range(1, n_chip):
            grad_copy(d, h).start()
        hand_copy(0, h).start()
    out_ref[...] = jnp.where(pre > 0, pre, low - 1.0).astype(BF16)
    out_copy = pltpu.make_async_copy(out_ref, out_hbm, out_sem.at[0])
    out_copy.start()

    def gw_copy(d):
        return to_col(gw_send.at[col_peer(d)], gw_recv.at[d], w_send, w_recv, d, col_peer(d))

    term = jnp.dot(gathered.T.astype(BF16), grad, preferred_element_type=F32)
    gw_send[...] = term.astype(gw_send.dtype).reshape(n_col, chunk, width)
    for d in range(1, n_col):
        gw_copy(d).start()

    def back_copy(d, h):
        return to_row(back_send.at[h, d], back_recv.at[h, d], b_send, b_recv, d, h)

    def half_product(start, count, side_core, h):
        at = pl.ds(pl.multiple_of(side_core * half, share), half)
        return jnp.dot(
            dense_t[rows_at(start, count), at], grad_all[h, at, :], preferred_element_type=F32)

    def backward(i, h):
        return (back_sum[h, rows_at(i * share, share), :]
                + half_product(i * share, share, 1 - core, h))

    def gwz_copy(d):
        return to_row(gwz_recv.at[my_r], gwz_recv.at[my_r], z_send, z_recv, d)

    for h in range(PARTS):
        def first_step(start, count):
            back_sum[h, rows_at(start, count), :] = half_product(start, count, core, h)

        def backward_send(i):
            d = i + 1
            back_send[h, d] = backward(row_peer(d), h).astype(BF16)
            back_copy(d, h).start()

        for d in range(1, n_chip):
            grad_copy(d, h).wait_recv()
            hand_copy(d, h).start()
        group(n_row, first_step)
        for d in range(n_chip):
            hand_copy(d, h).wait_recv()
        each(n_row - 1, backward_send)
        if h == 0:
            gw_sum = gw_send[my_c].astype(F32)
            for d in range(1, n_col):
                gw_copy(d).wait_recv()
                gw_sum = gw_sum + gw_recv[d].astype(F32)
            gwz_recv[my_r] = gw_sum.astype(gw_send.dtype)
            for d in range(1, n_row):
                gwz_copy(d).start()

    def gb_copy(d):
        return to_row(gb_recv.at[my_r], gb_recv.at[my_r], s_send, s_recv, d)

    ones = jnp.ones((16, n_col * share), BF16)
    for h in range(PARTS):
        gb_recv[my_r, :, lanes(h)] = jnp.dot(
            ones, grad_all[h], preferred_element_type=F32)[:8]
    for d in range(1, n_row):
        gb_copy(d).start()

    totals = [backward(my_r, h) for h in range(PARTS)]

    for d in range(1, n_row):
        gwz_copy(d).wait_recv()
    whole = gwz_recv[0].astype(F32)
    for i in range(1, n_row):
        whole = whole + gwz_recv[i].astype(F32)

    def all_copy(d):
        return to_col(gw_all.at[my_c], gw_all.at[my_c], a_send, a_recv, d, col_peer(d))

    gw_all[my_c] = whole.astype(gw_all.dtype)
    for d in range(1, n_col):
        all_copy(d).start()

    for h in range(PARTS):
        total = totals[h]
        for d in range(1, n_row):
            back_copy(d, h).wait_recv()
            total = total + back_recv[h, d].astype(F32)
        gmix_ref[:, lanes(h)] = total.astype(BF16)

    for d in range(1, n_row):
        gb_copy(d).wait_recv()
    gb_copy_out = pltpu.make_async_copy(gb_recv, gb_hbm, out_sem.at[1])
    gb_copy_out.start()

    for d in range(1, n_row):
        gwz_copy(d).wait_send()
        gb_copy(d).wait_send()
    for h in range(PARTS):
        for d in range(1, n_row):
            feat_copy(d, h).wait_send()
            back_copy(d, h).wait_send()
        for d in range(n_chip):
            pair_copy(d, h).wait_send()
            hand_copy(d, h).wait_send()
        for d in range(1, n_chip):
            part_copy(d, h).wait_send()
            grad_copy(d, h).wait_send()
    for d in range(1, n_col):
        all_copy(d).wait_recv()
    gw_copy_out = pltpu.make_async_copy(gw_all, gw_hbm, out_sem.at[2])
    gw_copy_out.start()
    for d in range(1, n_col):
        gw_copy(d).wait_send()
        all_copy(d).wait_send()
    out_copy.wait()
    gb_copy_out.wait()
    gw_copy_out.wait()


def finish(part_ref, gmix_ref, gwp_ref, gbp_ref, weight_ref, out_ref, gfeat_ref, gw_ref, gb_ref):
    out_ref[...] = part_ref[...]
    gfeat_ref[...] = lax.dot_general(
        gmix_ref[...], weight_ref[...], (((1,), (1,)), ((), ())),
        preferred_element_type=F32).astype(BF16)
    gw_ref[...] = gwp_ref[...].astype(F32).reshape(gw_ref.shape)
    gb = gbp_ref[0]
    for i in range(1, gbp_ref.shape[0]):
        gb = gb + gbp_ref[i]
    gb_ref[...] = gb[0:1]


def body(n_row, n_col, features, weight, bias, grad_out, tile_rows, tile_cols, tile_counts, tile_values):
    values = tile_values[0, 0]
    slots, side = values.shape[0], values.shape[1]
    share, width = features.shape
    row_tiles = share * n_col // side
    col_tiles = share * n_row // side
    chunk = width // n_col
    gw_type = BF16 if chunk % 16 == 0 else F32
    index_rows = -(-(2 + -(-(row_tiles * col_tiles) // slots)) // 8) * 8
    vmem = pl.BlockSpec(memory_space=pltpu.VMEM)
    smem = pl.BlockSpec(memory_space=pltpu.SMEM)
    anywhere = pl.BlockSpec(memory_space=pl.ANY)
    dma = pltpu.SemaphoreType.DMA
    part = width // PARTS
    row_sem, col_sem, chip_sem = dma((PARTS * n_row,)), dma((n_col,)), dma((PARTS * (n_col // 2),))
    buffers = [
        ((width, width), BF16),
        ((1, width), F32),
        ((share, width), BF16),
        ((1, slots), jnp.int32),
        ((1, slots), jnp.int32),
        ((share, width), BF16),
        ((slots, side, side), BF16),
        ((slots, side, side), BF16),
        ((row_tiles * side, col_tiles * side), BF16),
        ((col_tiles * side, row_tiles * side), BF16),
        ((PARTS, n_row, share, part), BF16),
        ((PARTS, n_col // 2 * share, part), BF16),
        ((PARTS, n_col // 2, share, part), BF16),
        ((PARTS, n_col // 2, share, part), BF16),
        ((PARTS, n_col // 2, share, part), BF16),
        ((PARTS, n_col * share, part), BF16),
        ((PARTS, n_col // 2 * share, part), F32),
        ((PARTS, n_row * share, part), F32),
        ((PARTS, n_row, share, part), BF16),
        ((PARTS, n_row, share, part), BF16),
        ((n_col, chunk, width), gw_type),
        ((n_col, chunk, width), gw_type),
        ((n_row, chunk, width), gw_type),
        ((n_col, chunk, width), gw_type),
        ((n_row, 8, width), F32),
        ((index_rows, slots), jnp.int32),
    ]
    out, gmix, gw, gb = pl.pallas_call(
        functools.partial(kernel, n_row, n_col, row_tiles, col_tiles),
        out_shape=(
            jax.ShapeDtypeStruct((share, width), BF16),
            jax.ShapeDtypeStruct((share, width), BF16),
            jax.ShapeDtypeStruct((n_col, chunk, width), gw_type),
            jax.ShapeDtypeStruct((n_row, 8, width), F32),
        ),
        in_specs=[anywhere] * 6 + [smem, anywhere],
        out_specs=(anywhere, vmem, anywhere, anywhere),
        scratch_shapes=[pltpu.VMEM(shape, kind) for shape, kind in buffers] + [
            pltpu.SMEM((index_rows, slots), jnp.int32),
            dma((CHUNKS,)), dma(()), dma((5 + PARTS,)), dma((3,)),
            row_sem, row_sem, chip_sem, chip_sem, chip_sem, chip_sem, chip_sem, chip_sem,
            chip_sem, chip_sem, row_sem, row_sem,
            col_sem, col_sem, row_sem, row_sem, col_sem, col_sem, row_sem, row_sem,
        ],
        compiler_params=pltpu.CompilerParams(
            collective_id=0, has_side_effects=True,
            vmem_limit_bytes=VMEM_BYTES),
        cost_estimate=pl.CostEstimate(
            flops=4 * row_tiles * col_tiles * side * side * width,
            bytes_accessed=2 * slots * side * side, transcendentals=share * width),
    )(features, weight, bias[None, :], grad_out, tile_rows[0], tile_cols[0], tile_counts, values)
    out, gfeat, gw, gb = pl.pallas_call(
        finish,
        out_shape=(
            jax.ShapeDtypeStruct((share, width), BF16),
            jax.ShapeDtypeStruct((share, width), BF16),
            jax.ShapeDtypeStruct((width, width), F32),
            jax.ShapeDtypeStruct((1, width), F32),
        ),
        in_specs=[vmem] * 5,
        out_specs=(vmem, vmem, vmem, vmem),
        compiler_params=pltpu.CompilerParams(vmem_limit_bytes=VMEM_BYTES),
    )(out, gmix, gw, gb, weight)
    return out, gfeat, gw, gb[0]


def solution(mesh):
    placed = (
        P(("col", "row"), None),
        P(),
        P(),
        P(("row", "col"), None),
        P("row", "col", None),
        P("row", "col", None),
        P("row", "col"),
        P("row", "col", None, None, None),
    )
    return jax.shard_map(
        functools.partial(body, mesh.shape["row"], mesh.shape["col"]),
        mesh=mesh,
        in_specs=placed,
        out_specs=(P(("row", "col"), None), P(("col", "row"), None), P(), P()),
        check_vma=False,
    )
```

```python
import functools

import jax
import jax.numpy as jnp
from jax import lax
from jax.experimental import pallas as pl
from jax.experimental.pallas import tpu as pltpu
from jax.sharding import PartitionSpec as P

MESH = pl.DeviceIdType.MESH
CHUNKS = 4
PARTS = 2
VMEM_BYTES = 60 * 2**20
F32 = jnp.float32
BF16 = jnp.bfloat16


def each(n, step):
    if n <= 8:
        for i in range(n):
            step(i)
    else:
        lax.fori_loop(0, n, lambda i, _: (step(i), 0)[1], 0)


def kernel(
    n_row, n_col, row_tiles, col_tiles,
    feat_ref, weight_hbm, bias_hbm, gout_hbm, rows_hbm, cols_hbm, count_ref, values_ref,
    out_hbm, gmix_ref, gw_hbm, gb_hbm,
    weight_ref, bias_ref, gout_ref, rows_ref, cols_ref, out_ref,
    vals, seq, dense, dense_t, feat_all, pair_send, pair_recv, part_send, part_recv, grad_all,
    own_sum, back_sum,
    back_send, back_recv, gw_send, gw_recv, gwz_recv, gw_all, gb_recv, idx_v, idx_s,
    val_sem, idx_sem, in_sem, out_sem, f_send, f_recv, p_send, p_recv, q_send, q_recv, g_send, g_recv,
    h_send, h_recv, b_send, b_recv,
    w_send, w_recv, z_send, z_recv, a_send, a_recv, s_send, s_recv,
):
    my_r = lax.axis_index("row")
    my_c = lax.axis_index("col")
    n_chip = n_col // 2
    core, chip = lax.rem(my_c, 2), my_c // 2
    sibling = my_c + 1 - 2 * core
    slots, side = vals.shape[0], vals.shape[1]
    share, width = feat_ref.shape
    per = slots // CHUNKS
    chunk = width // n_col
    part = width // PARTS

    def lanes(h):
        return slice(h * part, (h + 1) * part)

    row_order, chip_order = list(range(1, n_row)), list(range(1, n_chip))
    if n_row == 4:
        turned = 2 * lax.rem(my_r, 2)
        row_order = [2, 3 - turned, 1 + turned]
    if n_chip == 4:
        turned = 2 * lax.rem(chip, 2)
        chip_order = [3 - turned, 2, 1 + turned]

    def row_peer(d):
        return lax.rem(my_r + d, n_row)

    def col_peer(d):
        return lax.rem(my_c + d, n_col)

    def chip_peer(d):
        return 2 * lax.rem(chip + d, n_chip) + core

    def to_row(src, dst, send, recv, d, h=0):
        return pltpu.make_async_remote_copy(
            src_ref=src, dst_ref=dst, send_sem=send.at[h * n_row + d], recv_sem=recv.at[h * n_row + d],
            device_id=(row_peer(d), my_c), device_id_type=MESH)

    def to_col(src, dst, send, recv, d, peer, h=0):
        return pltpu.make_async_remote_copy(
            src_ref=src, dst_ref=dst, send_sem=send.at[h * n_chip + d], recv_sem=recv.at[h * n_chip + d],
            device_id=(my_r, peer), device_id_type=MESH)

    def fetch(q):
        return pltpu.make_async_copy(
            values_ref.at[pl.ds(q * per, per)], vals.at[pl.ds(q * per, per)], val_sem.at[q])

    bring = [
        pltpu.make_async_copy(src, dst, in_sem.at[i])
        for i, (src, dst) in enumerate((
            (rows_hbm, rows_ref), (cols_hbm, cols_ref), (weight_hbm, weight_ref),
            (bias_hbm, bias_ref), (gout_hbm, gout_ref),
            *((feat_ref.at[:, lanes(h)], feat_all.at[h, my_r]) for h in range(PARTS))))
    ]
    bring[0].start()
    bring[1].start()
    for q in range(CHUNKS):
        fetch(q).start()
    for copy in bring[2:]:
        copy.start()

    barrier = pltpu.get_barrier_semaphore()
    for d in range(1, n_row):
        pl.semaphore_signal(barrier, inc=1, device_id=(row_peer(d), my_c), device_id_type=MESH)
    for d in range(1, n_col):
        pl.semaphore_signal(barrier, inc=1, device_id=(my_r, col_peer(d)), device_id_type=MESH)

    pl.semaphore_wait(barrier, n_row + n_col - 2)

    def feat_copy(d, h):
        return to_row(feat_ref.at[:, lanes(h)], feat_all.at[h, my_r], f_send, f_recv, d, h)

    for h in range(PARTS):
        for d in row_order:
            feat_copy(d, h).start()

    tiles = row_tiles * col_tiles
    lane = lax.broadcasted_iota(jnp.int32, (slots, slots), 1)
    sub = lax.broadcasted_iota(jnp.int32, (slots, slots), 0)
    live = lane < count_ref[0, 0]
    bring[0].wait()
    bring[1].wait()
    key = jnp.where(
        live, jnp.broadcast_to(rows_ref[...] * col_tiles + cols_ref[...], (slots, slots)), tiles)
    key_t = key.T
    ahead = (key_t < key) | ((key_t == key) & (sub < lane))
    rank = jnp.sum(ahead.astype(jnp.int32), axis=0, keepdims=True)
    hit = jnp.broadcast_to(rank, (slots, slots)).T == lane
    idx_v[0:1, :] = jnp.sum(jnp.where(hit, sub, 0), axis=0, keepdims=True)
    idx_v[1:2, :] = jnp.sum(jnp.where(hit, key_t, 0), axis=0, keepdims=True)
    for q in range(-(-tiles // slots)):
        upto = (key_t <= lane + q * slots).astype(jnp.int32)
        idx_v[2 + q : 3 + q, :] = jnp.sum(upto, axis=0, keepdims=True)
    idx_copy = pltpu.make_async_copy(idx_v, idx_s, idx_sem)
    idx_copy.start()


    idx_copy.wait()
    for q in range(CHUNKS):
        fetch(q).wait()

    def add_slot(i, acc):
        same = (i > 0) & (idx_s[1, i] == idx_s[1, jnp.maximum(i - 1, 0)])
        keep = jnp.where(same, 1.0, 0.0).astype(F32)
        acc = acc * keep + vals[idx_s[0, i]].astype(F32)
        seq[i] = acc.astype(BF16)
        return acc

    lax.fori_loop(0, slots, add_slot, jnp.zeros((side, side), F32), unroll=8)

    def dense_tile(r, c):
        k = r * col_tiles + c
        before = jnp.maximum(k - 1, 0)
        end = idx_s[2 + k // slots, lax.rem(k, slots)]
        start = jnp.where(k > 0, idx_s[2 + before // slots, lax.rem(before, slots)], 0)
        some = jnp.where(end > start, 1.0, 0.0).astype(F32)
        return (seq[jnp.maximum(end - 1, 0)].astype(F32) * some).astype(BF16)

    tiles_per = share // side

    def place(r, _):
        block, inner = r // tiles_per, lax.rem(r, tiles_per)
        at = (lax.rem(block, 2) * n_chip + block // 2) * tiles_per + inner
        for c in range(col_tiles):
            dense[pl.ds(pl.multiple_of(at * side, side), side), c * side : (c + 1) * side] = (
                dense_tile(r, c))
        return 0

    lax.fori_loop(0, row_tiles, place, 0)

    for copy in bring[2:]:
        copy.wait()
    half = n_chip * share

    def group(n, step):
        size = 4 if n % 4 == 0 else 1
        each(n // size, lambda g: step(g * size * share, size * share))

    def rows_at(start, count):
        return pl.ds(pl.multiple_of(start, share), count)

    def aggregate(start, count, h):
        return jnp.dot(
            dense[rows_at(start, count), :], feat_all[h].reshape(n_row * share, part),
            preferred_element_type=F32)

    def chip_rows(d):
        return rows_at(lax.rem(chip + d, n_chip) * share, share)

    def pair_copy(d, h):
        return to_col(
            pair_send.at[h, chip_rows(d), :], pair_recv.at[h, d], p_send, p_recv, d, sibling, h)

    def part_copy(d, h):
        return to_col(
            part_send.at[h, d], part_recv.at[h, d], q_send, q_recv, d, chip_peer(d), h)

    for h in range(PARTS):
        def pair_step(start, count):
            pair_send[h, rows_at(start, count), :] = (
                aggregate((1 - core) * half + start, count, h).astype(BF16))

        def own_step(start, count):
            own_sum[h, rows_at(start, count), :] = aggregate(core * half + start, count, h)

        for d in range(1, n_row):
            feat_copy(d, h).wait_recv()
        group(n_chip, pair_step)
        for d in chip_order:
            pair_copy(d, h).start()
        pair_copy(0, h).start()
        group(n_chip, own_step)
        for d in chip_order:
            pair_copy(d, h).wait_recv()
            part_send[h, d] = (
                own_sum[h, chip_rows(d), :] + pair_recv[h, d].astype(F32)).astype(BF16)
            part_copy(d, h).start()
        pair_copy(0, h).wait_recv()

    def turn(r, _):
        for c in range(col_tiles):
            tile = dense[pl.ds(pl.multiple_of(r * side, side), side), c * side : (c + 1) * side]
            dense_t[c * side : (c + 1) * side, pl.ds(pl.multiple_of(r * side, side), side)] = (
                tile.astype(F32).T.astype(BF16))
        return 0

    lax.fori_loop(0, row_tiles, turn, 0)

    sums = []
    for h in range(PARTS):
        total = own_sum[h, chip_rows(0), :] + pair_recv[h, 0].astype(F32)
        for d in range(1, n_chip):
            part_copy(d, h).wait_recv()
            total = total + part_recv[h, d].astype(F32)
        sums.append(total)
    gathered = jnp.concatenate(sums, axis=1)

    pre = jnp.dot(
        gathered.astype(BF16), weight_ref[...], preferred_element_type=F32) + bias_ref[...]
    low = jnp.exp(jnp.minimum(pre, 0.0))
    grad = (gout_ref[...].astype(F32) * jnp.where(pre > 0, 1.0, low)).astype(BF16)

    def rows_of(block, h):
        return grad_all.at[h, rows_at(block * share, share), :]

    mine_at = core * n_chip + chip
    for h in range(PARTS):
        grad_all[h, rows_at(mine_at * share, share), :] = grad[:, lanes(h)]

    def grad_copy(d, h):
        return to_col(
            rows_of(mine_at, h), rows_of(mine_at, h), g_send, g_recv, d, chip_peer(d), h)

    def hand_copy(d, h):
        at = core * n_chip + lax.rem(chip + n_chip - d, n_chip)
        return to_col(rows_of(at, h), rows_of(at, h), h_send, h_recv, d, sibling, h)

    for h in range(PARTS):
        for d in chip_order:
            grad_copy(d, h).start()
        hand_copy(0, h).start()
    out_ref[...] = jnp.where(pre > 0, pre, low - 1.0).astype(BF16)
    out_copy = pltpu.make_async_copy(out_ref, out_hbm, out_sem.at[0])
    out_copy.start()

    def gw_copy(d):
        return to_col(gw_send.at[col_peer(d)], gw_recv.at[d], w_send, w_recv, d, col_peer(d))

    term = jnp.dot(gathered.T.astype(BF16), grad, preferred_element_type=F32)
    gw_send[...] = term.astype(gw_send.dtype).reshape(n_col, chunk, width)
    for d in range(1, n_col):
        gw_copy(d).start()

    def back_copy(d, h):
        return to_row(back_send.at[h, d], back_recv.at[h, d], b_send, b_recv, d, h)

    def half_product(start, count, side_core, h):
        at = pl.ds(pl.multiple_of(side_core * half, share), half)
        return jnp.dot(
            dense_t[rows_at(start, count), at], grad_all[h, at, :], preferred_element_type=F32)

    def backward(i, h):
        return (back_sum[h, rows_at(i * share, share), :]
                + half_product(i * share, share, 1 - core, h))

    def gwz_copy(d):
        return to_row(gwz_recv.at[my_r], gwz_recv.at[my_r], z_send, z_recv, d)

    for h in range(PARTS):
        def first_step(start, count):
            back_sum[h, rows_at(start, count), :] = half_product(start, count, core, h)

        def backward_send(d):
            back_send[h, d] = backward(row_peer(d), h).astype(BF16)
            back_copy(d, h).start()

        for d in range(1, n_chip):
            grad_copy(d, h).wait_recv()
            hand_copy(d, h).start()
        group(n_row, first_step)
        for d in range(n_chip):
            hand_copy(d, h).wait_recv()
        if n_row <= 8:
            for d in row_order:
                backward_send(d)
        else:
            each(n_row - 1, lambda i: backward_send(i + 1))
        if h == 0:
            gw_sum = gw_send[my_c].astype(F32)
            for d in range(1, n_col):
                gw_copy(d).wait_recv()
                gw_sum = gw_sum + gw_recv[d].astype(F32)
            gwz_recv[my_r] = gw_sum.astype(gw_send.dtype)
            for d in range(1, n_row):
                gwz_copy(d).start()

    def gb_copy(d):
        return to_row(gb_recv.at[my_r], gb_recv.at[my_r], s_send, s_recv, d)

    ones = jnp.ones((16, n_col * share), BF16)
    for h in range(PARTS):
        gb_recv[my_r, :, lanes(h)] = jnp.dot(
            ones, grad_all[h], preferred_element_type=F32)[:8]
    for d in range(1, n_row):
        gb_copy(d).start()

    totals = [backward(my_r, h) for h in range(PARTS)]

    for d in range(1, n_row):
        gwz_copy(d).wait_recv()
    whole = gwz_recv[0].astype(F32)
    for i in range(1, n_row):
        whole = whole + gwz_recv[i].astype(F32)

    def all_copy(d):
        return to_col(gw_all.at[my_c], gw_all.at[my_c], a_send, a_recv, d, col_peer(d))

    gw_all[my_c] = whole.astype(gw_all.dtype)
    for d in range(1, n_col):
        all_copy(d).start()

    for h in range(PARTS):
        total = totals[h]
        for d in range(1, n_row):
            back_copy(d, h).wait_recv()
            total = total + back_recv[h, d].astype(F32)
        gmix_ref[:, lanes(h)] = total.astype(BF16)

    for d in range(1, n_row):
        gb_copy(d).wait_recv()
    gb_copy_out = pltpu.make_async_copy(gb_recv, gb_hbm, out_sem.at[1])
    gb_copy_out.start()

    for d in range(1, n_row):
        gwz_copy(d).wait_send()
        gb_copy(d).wait_send()
    for h in range(PARTS):
        for d in range(1, n_row):
            feat_copy(d, h).wait_send()
            back_copy(d, h).wait_send()
        for d in range(n_chip):
            pair_copy(d, h).wait_send()
            hand_copy(d, h).wait_send()
        for d in range(1, n_chip):
            part_copy(d, h).wait_send()
            grad_copy(d, h).wait_send()
    for d in range(1, n_col):
        all_copy(d).wait_recv()
    gw_copy_out = pltpu.make_async_copy(gw_all, gw_hbm, out_sem.at[2])
    gw_copy_out.start()
    for d in range(1, n_col):
        gw_copy(d).wait_send()
        all_copy(d).wait_send()
    out_copy.wait()
    gb_copy_out.wait()
    gw_copy_out.wait()


def finish(part_ref, gmix_ref, gwp_ref, gbp_ref, weight_ref, out_ref, gfeat_ref, gw_ref, gb_ref):
    out_ref[...] = part_ref[...]
    gfeat_ref[...] = lax.dot_general(
        gmix_ref[...], weight_ref[...], (((1,), (1,)), ((), ())),
        preferred_element_type=F32).astype(BF16)
    gw_ref[...] = gwp_ref[...].astype(F32).reshape(gw_ref.shape)
    gb = gbp_ref[0]
    for i in range(1, gbp_ref.shape[0]):
        gb = gb + gbp_ref[i]
    gb_ref[...] = gb[0:1]


def body(n_row, n_col, features, weight, bias, grad_out, tile_rows, tile_cols, tile_counts, tile_values):
    values = tile_values[0, 0]
    slots, side = values.shape[0], values.shape[1]
    share, width = features.shape
    row_tiles = share * n_col // side
    col_tiles = share * n_row // side
    chunk = width // n_col
    gw_type = BF16 if chunk % 16 == 0 else F32
    index_rows = -(-(2 + -(-(row_tiles * col_tiles) // slots)) // 8) * 8
    vmem = pl.BlockSpec(memory_space=pltpu.VMEM)
    smem = pl.BlockSpec(memory_space=pltpu.SMEM)
    anywhere = pl.BlockSpec(memory_space=pl.ANY)
    dma = pltpu.SemaphoreType.DMA
    part = width // PARTS
    row_sem, col_sem, chip_sem = dma((PARTS * n_row,)), dma((n_col,)), dma((PARTS * (n_col // 2),))
    buffers = [
        ((width, width), BF16),
        ((1, width), F32),
        ((share, width), BF16),
        ((1, slots), jnp.int32),
        ((1, slots), jnp.int32),
        ((share, width), BF16),
        ((slots, side, side), BF16),
        ((slots, side, side), BF16),
        ((row_tiles * side, col_tiles * side), BF16),
        ((col_tiles * side, row_tiles * side), BF16),
        ((PARTS, n_row, share, part), BF16),
        ((PARTS, n_col // 2 * share, part), BF16),
        ((PARTS, n_col // 2, share, part), BF16),
        ((PARTS, n_col // 2, share, part), BF16),
        ((PARTS, n_col // 2, share, part), BF16),
        ((PARTS, n_col * share, part), BF16),
        ((PARTS, n_col // 2 * share, part), F32),
        ((PARTS, n_row * share, part), F32),
        ((PARTS, n_row, share, part), BF16),
        ((PARTS, n_row, share, part), BF16),
        ((n_col, chunk, width), gw_type),
        ((n_col, chunk, width), gw_type),
        ((n_row, chunk, width), gw_type),
        ((n_col, chunk, width), gw_type),
        ((n_row, 8, width), F32),
        ((index_rows, slots), jnp.int32),
    ]
    out, gmix, gw, gb = pl.pallas_call(
        functools.partial(kernel, n_row, n_col, row_tiles, col_tiles),
        out_shape=(
            jax.ShapeDtypeStruct((share, width), BF16),
            jax.ShapeDtypeStruct((share, width), BF16),
            jax.ShapeDtypeStruct((n_col, chunk, width), gw_type),
            jax.ShapeDtypeStruct((n_row, 8, width), F32),
        ),
        in_specs=[anywhere] * 6 + [smem, anywhere],
        out_specs=(anywhere, vmem, anywhere, anywhere),
        scratch_shapes=[pltpu.VMEM(shape, kind) for shape, kind in buffers] + [
            pltpu.SMEM((index_rows, slots), jnp.int32),
            dma((CHUNKS,)), dma(()), dma((5 + PARTS,)), dma((3,)),
            row_sem, row_sem, chip_sem, chip_sem, chip_sem, chip_sem, chip_sem, chip_sem,
            chip_sem, chip_sem, row_sem, row_sem,
            col_sem, col_sem, row_sem, row_sem, col_sem, col_sem, row_sem, row_sem,
        ],
        compiler_params=pltpu.CompilerParams(
            collective_id=0, has_side_effects=True,
            vmem_limit_bytes=VMEM_BYTES),
        cost_estimate=pl.CostEstimate(
            flops=4 * row_tiles * col_tiles * side * side * width,
            bytes_accessed=2 * slots * side * side, transcendentals=share * width),
    )(features, weight, bias[None, :], grad_out, tile_rows[0], tile_cols[0], tile_counts, values)
    out, gfeat, gw, gb = pl.pallas_call(
        finish,
        out_shape=(
            jax.ShapeDtypeStruct((share, width), BF16),
            jax.ShapeDtypeStruct((share, width), BF16),
            jax.ShapeDtypeStruct((width, width), F32),
            jax.ShapeDtypeStruct((1, width), F32),
        ),
        in_specs=[vmem] * 5,
        out_specs=(vmem, vmem, vmem, vmem),
        compiler_params=pltpu.CompilerParams(vmem_limit_bytes=VMEM_BYTES),
    )(out, gmix, gw, gb, weight)
    return out, gfeat, gw, gb[0]


def solution(mesh):
    placed = (
        P(("col", "row"), None),
        P(),
        P(),
        P(("row", "col"), None),
        P("row", "col", None),
        P("row", "col", None),
        P("row", "col"),
        P("row", "col", None, None, None),
    )
    return jax.shard_map(
        functools.partial(body, mesh.shape["row"], mesh.shape["col"]),
        mesh=mesh,
        in_specs=placed,
        out_specs=(P(("row", "col"), None), P(("col", "row"), None), P(), P()),
        check_vma=False,
    )
```

```python
import functools

import jax
import jax.numpy as jnp
from jax import lax
from jax.experimental import pallas as pl
from jax.experimental.pallas import tpu as pltpu
from jax.sharding import PartitionSpec as P

MESH = pl.DeviceIdType.MESH
CHUNKS = 4
PARTS = 2
VMEM_BYTES = 60 * 2**20
F32 = jnp.float32
BF16 = jnp.bfloat16


def each(n, step):
    if n <= 8:
        for i in range(n):
            step(i)
    else:
        lax.fori_loop(0, n, lambda i, _: (step(i), 0)[1], 0)


def kernel(
    n_row, n_col, row_tiles, col_tiles,
    feat_ref, weight_hbm, bias_hbm, gout_hbm, rows_hbm, cols_hbm, count_ref, values_ref,
    out_hbm, gmix_ref, gw_hbm, gb_hbm,
    weight_ref, bias_ref, gout_ref, rows_ref, cols_ref, out_ref,
    vals, seq, dense, dense_t, feat_all, pair_send, pair_recv, part_send, part_recv, grad_all,
    own_sum, back_sum,
    back_send, back_recv, gw_send, gw_recv, gwz_recv, gw_all, gb_recv, idx_v, idx_s,
    val_sem, idx_sem, in_sem, out_sem, f_send, f_recv, p_send, p_recv, q_send, q_recv, g_send, g_recv,
    h_send, h_recv, b_send, b_recv,
    w_send, w_recv, z_send, z_recv, a_send, a_recv, s_send, s_recv,
):
    my_r = lax.axis_index("row")
    my_c = lax.axis_index("col")
    n_chip = n_col // 2
    core, chip = lax.rem(my_c, 2), my_c // 2
    sibling = my_c + 1 - 2 * core
    slots, side = vals.shape[0], vals.shape[1]
    share, width = feat_ref.shape
    per = slots // CHUNKS
    chunk = width // n_col
    part = width // PARTS

    def lanes(h):
        return slice(h * part, (h + 1) * part)

    def row_peer(d):
        return lax.rem(my_r + d, n_row)

    def col_peer(d):
        return lax.rem(my_c + d, n_col)

    def chip_peer(d):
        return 2 * lax.rem(chip + d, n_chip) + core

    def to_row(src, dst, send, recv, d, h=0):
        return pltpu.make_async_remote_copy(
            src_ref=src, dst_ref=dst, send_sem=send.at[h * n_row + d], recv_sem=recv.at[h * n_row + d],
            device_id=(row_peer(d), my_c), device_id_type=MESH)

    def to_col(src, dst, send, recv, d, peer, h=0):
        return pltpu.make_async_remote_copy(
            src_ref=src, dst_ref=dst, send_sem=send.at[h * n_chip + d], recv_sem=recv.at[h * n_chip + d],
            device_id=(my_r, peer), device_id_type=MESH)

    def fetch(q):
        return pltpu.make_async_copy(
            values_ref.at[pl.ds(q * per, per)], vals.at[pl.ds(q * per, per)], val_sem.at[q])

    bring = [
        pltpu.make_async_copy(src, dst, in_sem.at[i])
        for i, (src, dst) in enumerate((
            (rows_hbm, rows_ref), (cols_hbm, cols_ref), (weight_hbm, weight_ref),
            (bias_hbm, bias_ref), (gout_hbm, gout_ref),
            *((feat_ref.at[:, lanes(h)], feat_all.at[h, my_r]) for h in range(PARTS))))
    ]
    bring[0].start()
    bring[1].start()
    for q in range(CHUNKS):
        fetch(q).start()
    for copy in bring[2:]:
        copy.start()

    barrier = pltpu.get_barrier_semaphore()
    for d in range(1, n_row):
        pl.semaphore_signal(barrier, inc=1, device_id=(row_peer(d), my_c), device_id_type=MESH)
    for d in range(1, n_col):
        pl.semaphore_signal(barrier, inc=1, device_id=(my_r, col_peer(d)), device_id_type=MESH)

    pl.semaphore_wait(barrier, n_row + n_col - 2)

    def feat_copy(d, h):
        return to_row(feat_ref.at[:, lanes(h)], feat_all.at[h, my_r], f_send, f_recv, d, h)

    for h in range(PARTS):
        for d in sorted(range(1, n_row), key=lambda d: abs(2 * d - n_row)):
            feat_copy(d, h).start()

    tiles = row_tiles * col_tiles
    lane = lax.broadcasted_iota(jnp.int32, (slots, slots), 1)
    sub = lax.broadcasted_iota(jnp.int32, (slots, slots), 0)
    live = lane < count_ref[0, 0]
    bring[0].wait()
    bring[1].wait()
    key = jnp.where(
        live, jnp.broadcast_to(rows_ref[...] * col_tiles + cols_ref[...], (slots, slots)), tiles)
    key_t = key.T
    ahead = (key_t < key) | ((key_t == key) & (sub < lane))
    rank = jnp.sum(ahead.astype(jnp.int32), axis=0, keepdims=True)
    hit = jnp.broadcast_to(rank, (slots, slots)).T == lane
    idx_v[0:1, :] = jnp.sum(jnp.where(hit, sub, 0), axis=0, keepdims=True)
    idx_v[1:2, :] = jnp.sum(jnp.where(hit, key_t, 0), axis=0, keepdims=True)
    for q in range(-(-tiles // slots)):
        upto = (key_t <= lane + q * slots).astype(jnp.int32)
        idx_v[2 + q : 3 + q, :] = jnp.sum(upto, axis=0, keepdims=True)
    idx_copy = pltpu.make_async_copy(idx_v, idx_s, idx_sem)
    idx_copy.start()


    idx_copy.wait()
    for q in range(CHUNKS):
        fetch(q).wait()

    def add_slot(i, acc):
        same = (i > 0) & (idx_s[1, i] == idx_s[1, jnp.maximum(i - 1, 0)])
        keep = jnp.where(same, 1.0, 0.0).astype(F32)
        acc = acc * keep + vals[idx_s[0, i]].astype(F32)
        seq[i] = acc.astype(BF16)
        return acc

    lax.fori_loop(0, slots, add_slot, jnp.zeros((side, side), F32), unroll=8)

    def dense_tile(r, c):
        k = r * col_tiles + c
        before = jnp.maximum(k - 1, 0)
        end = idx_s[2 + k // slots, lax.rem(k, slots)]
        start = jnp.where(k > 0, idx_s[2 + before // slots, lax.rem(before, slots)], 0)
        some = jnp.where(end > start, 1.0, 0.0).astype(F32)
        return (seq[jnp.maximum(end - 1, 0)].astype(F32) * some).astype(BF16)

    tiles_per = share // side

    def place(r, _):
        block, inner = r // tiles_per, lax.rem(r, tiles_per)
        at = (lax.rem(block, 2) * n_chip + block // 2) * tiles_per + inner
        for c in range(col_tiles):
            dense[pl.ds(pl.multiple_of(at * side, side), side), c * side : (c + 1) * side] = (
                dense_tile(r, c))
        return 0

    lax.fori_loop(0, row_tiles, place, 0)

    for copy in bring[2:]:
        copy.wait()
    half = n_chip * share

    def group(n, step):
        size = 4 if n % 4 == 0 else 1
        each(n // size, lambda g: step(g * size * share, size * share))

    def rows_at(start, count):
        return pl.ds(pl.multiple_of(start, share), count)

    def aggregate(start, count, h):
        return jnp.dot(
            dense[rows_at(start, count), :], feat_all[h].reshape(n_row * share, part),
            preferred_element_type=F32)

    def chip_rows(d):
        return rows_at(lax.rem(chip + d, n_chip) * share, share)

    def pair_copy(d, h):
        return to_col(
            pair_send.at[h, chip_rows(d), :], pair_recv.at[h, d], p_send, p_recv, d, sibling, h)

    def part_copy(d, h):
        return to_col(
            part_send.at[h, d], part_recv.at[h, d], q_send, q_recv, d, chip_peer(d), h)

    for h in range(PARTS):
        def pair_step(start, count):
            pair_send[h, rows_at(start, count), :] = (
                aggregate((1 - core) * half + start, count, h).astype(BF16))

        def own_step(start, count):
            own_sum[h, rows_at(start, count), :] = aggregate(core * half + start, count, h)

        for d in range(1, n_row):
            feat_copy(d, h).wait_recv()
        group(n_chip, pair_step)
        for d in range(n_chip):
            pair_copy((d + 1) % n_chip, h).start()
        group(n_chip, own_step)
        for d in range(1, n_chip):
            pair_copy(d, h).wait_recv()
            part_send[h, d] = (
                own_sum[h, chip_rows(d), :] + pair_recv[h, d].astype(F32)).astype(BF16)
            part_copy(d, h).start()
        pair_copy(0, h).wait_recv()

    def turn(r, _):
        for c in range(col_tiles):
            tile = dense[pl.ds(pl.multiple_of(r * side, side), side), c * side : (c + 1) * side]
            dense_t[c * side : (c + 1) * side, pl.ds(pl.multiple_of(r * side, side), side)] = (
                tile.astype(F32).T.astype(BF16))
        return 0

    lax.fori_loop(0, row_tiles, turn, 0)

    sums = []
    for h in range(PARTS):
        total = own_sum[h, chip_rows(0), :] + pair_recv[h, 0].astype(F32)
        for d in range(1, n_chip):
            part_copy(d, h).wait_recv()
            total = total + part_recv[h, d].astype(F32)
        sums.append(total)
    gathered = jnp.concatenate(sums, axis=1)

    pre = jnp.dot(
        gathered.astype(BF16), weight_ref[...], preferred_element_type=F32) + bias_ref[...]
    low = jnp.exp(jnp.minimum(pre, 0.0))
    grad = (gout_ref[...].astype(F32) * jnp.where(pre > 0, 1.0, low)).astype(BF16)

    def rows_of(block, h):
        return grad_all.at[h, rows_at(block * share, share), :]

    mine_at = core * n_chip + chip
    for h in range(PARTS):
        grad_all[h, rows_at(mine_at * share, share), :] = grad[:, lanes(h)]

    def grad_copy(d, h):
        return to_col(
            rows_of(mine_at, h), rows_of(mine_at, h), g_send, g_recv, d, chip_peer(d), h)

    def hand_copy(d, h):
        at = core * n_chip + lax.rem(chip + n_chip - d, n_chip)
        return to_col(rows_of(at, h), rows_of(at, h), h_send, h_recv, d, sibling, h)

    for h in range(PARTS):
        for d in range(1, n_chip):
            grad_copy(d, h).start()
        hand_copy(0, h).start()
    out_ref[...] = jnp.where(pre > 0, pre, low - 1.0).astype(BF16)
    out_copy = pltpu.make_async_copy(out_ref, out_hbm, out_sem.at[0])
    out_copy.start()

    def gw_copy(d):
        return to_col(gw_send.at[col_peer(d)], gw_recv.at[d], w_send, w_recv, d, col_peer(d))

    term = jnp.dot(gathered.T.astype(BF16), grad, preferred_element_type=F32)
    gw_send[...] = term.astype(gw_send.dtype).reshape(n_col, chunk, width)
    for d in range(1, n_col):
        gw_copy(d).start()

    def back_copy(d, h):
        return to_row(back_send.at[h, d], back_recv.at[h, d], b_send, b_recv, d, h)

    def half_product(start, count, side_core, h):
        at = pl.ds(pl.multiple_of(side_core * half, share), half)
        return jnp.dot(
            dense_t[rows_at(start, count), at], grad_all[h, at, :], preferred_element_type=F32)

    def backward(i, h):
        return (back_sum[h, rows_at(i * share, share), :]
                + half_product(i * share, share, 1 - core, h))

    def gwz_copy(d):
        return to_row(gwz_recv.at[my_r], gwz_recv.at[my_r], z_send, z_recv, d)

    for h in range(PARTS):
        def first_step(start, count):
            back_sum[h, rows_at(start, count), :] = half_product(start, count, core, h)

        def backward_send(i):
            d = i + 1
            back_send[h, d] = backward(row_peer(d), h).astype(BF16)
            back_copy(d, h).start()

        for d in range(1, n_chip):
            grad_copy(d, h).wait_recv()
            hand_copy(d, h).start()
        group(n_row, first_step)
        for d in range(n_chip):
            hand_copy(d, h).wait_recv()
        each(n_row - 1, backward_send)
        if h == 0:
            gw_sum = gw_send[my_c].astype(F32)
            for d in range(1, n_col):
                gw_copy(d).wait_recv()
                gw_sum = gw_sum + gw_recv[d].astype(F32)
            gwz_recv[my_r] = gw_sum.astype(gw_send.dtype)
            for d in range(1, n_row):
                gwz_copy(d).start()

    def gb_copy(d):
        return to_row(gb_recv.at[my_r], gb_recv.at[my_r], s_send, s_recv, d)

    ones = jnp.ones((16, n_col * share), BF16)
    for h in range(PARTS):
        gb_recv[my_r, :, lanes(h)] = jnp.dot(
            ones, grad_all[h], preferred_element_type=F32)[:8]
    for d in range(1, n_row):
        gb_copy(d).start()

    totals = [backward(my_r, h) for h in range(PARTS)]

    for d in range(1, n_row):
        gwz_copy(d).wait_recv()
    whole = gwz_recv[0].astype(F32)
    for i in range(1, n_row):
        whole = whole + gwz_recv[i].astype(F32)

    def all_copy(d):
        return to_col(gw_all.at[my_c], gw_all.at[my_c], a_send, a_recv, d, col_peer(d))

    gw_all[my_c] = whole.astype(gw_all.dtype)
    for d in range(1, n_col):
        all_copy(d).start()

    for h in range(PARTS):
        total = totals[h]
        for d in range(1, n_row):
            back_copy(d, h).wait_recv()
            total = total + back_recv[h, d].astype(F32)
        gmix_ref[:, lanes(h)] = total.astype(BF16)

    for d in range(1, n_row):
        gb_copy(d).wait_recv()
    gb_copy_out = pltpu.make_async_copy(gb_recv, gb_hbm, out_sem.at[1])
    gb_copy_out.start()

    for d in range(1, n_row):
        gwz_copy(d).wait_send()
        gb_copy(d).wait_send()
    for h in range(PARTS):
        for d in range(1, n_row):
            feat_copy(d, h).wait_send()
            back_copy(d, h).wait_send()
        for d in range(n_chip):
            pair_copy(d, h).wait_send()
            hand_copy(d, h).wait_send()
        for d in range(1, n_chip):
            part_copy(d, h).wait_send()
            grad_copy(d, h).wait_send()
    for d in range(1, n_col):
        all_copy(d).wait_recv()
    gw_copy_out = pltpu.make_async_copy(gw_all, gw_hbm, out_sem.at[2])
    gw_copy_out.start()
    for d in range(1, n_col):
        gw_copy(d).wait_send()
        all_copy(d).wait_send()
    out_copy.wait()
    gb_copy_out.wait()
    gw_copy_out.wait()


def finish(part_ref, gmix_ref, gwp_ref, gbp_ref, weight_ref, out_ref, gfeat_ref, gw_ref, gb_ref):
    out_ref[...] = part_ref[...]
    gfeat_ref[...] = lax.dot_general(
        gmix_ref[...], weight_ref[...], (((1,), (1,)), ((), ())),
        preferred_element_type=F32).astype(BF16)
    gw_ref[...] = gwp_ref[...].astype(F32).reshape(gw_ref.shape)
    gb = gbp_ref[0]
    for i in range(1, gbp_ref.shape[0]):
        gb = gb + gbp_ref[i]
    gb_ref[...] = gb[0:1]


def body(n_row, n_col, features, weight, bias, grad_out, tile_rows, tile_cols, tile_counts, tile_values):
    values = tile_values[0, 0]
    slots, side = values.shape[0], values.shape[1]
    share, width = features.shape
    row_tiles = share * n_col // side
    col_tiles = share * n_row // side
    chunk = width // n_col
    gw_type = BF16 if chunk % 16 == 0 else F32
    index_rows = -(-(2 + -(-(row_tiles * col_tiles) // slots)) // 8) * 8
    vmem = pl.BlockSpec(memory_space=pltpu.VMEM)
    smem = pl.BlockSpec(memory_space=pltpu.SMEM)
    anywhere = pl.BlockSpec(memory_space=pl.ANY)
    dma = pltpu.SemaphoreType.DMA
    part = width // PARTS
    row_sem, col_sem, chip_sem = dma((PARTS * n_row,)), dma((n_col,)), dma((PARTS * (n_col // 2),))
    buffers = [
        ((width, width), BF16),
        ((1, width), F32),
        ((share, width), BF16),
        ((1, slots), jnp.int32),
        ((1, slots), jnp.int32),
        ((share, width), BF16),
        ((slots, side, side), BF16),
        ((slots, side, side), BF16),
        ((row_tiles * side, col_tiles * side), BF16),
        ((col_tiles * side, row_tiles * side), BF16),
        ((PARTS, n_row, share, part), BF16),
        ((PARTS, n_col // 2 * share, part), BF16),
        ((PARTS, n_col // 2, share, part), BF16),
        ((PARTS, n_col // 2, share, part), BF16),
        ((PARTS, n_col // 2, share, part), BF16),
        ((PARTS, n_col * share, part), BF16),
        ((PARTS, n_col // 2 * share, part), F32),
        ((PARTS, n_row * share, part), F32),
        ((PARTS, n_row, share, part), BF16),
        ((PARTS, n_row, share, part), BF16),
        ((n_col, chunk, width), gw_type),
        ((n_col, chunk, width), gw_type),
        ((n_row, chunk, width), gw_type),
        ((n_col, chunk, width), gw_type),
        ((n_row, 8, width), F32),
        ((index_rows, slots), jnp.int32),
    ]
    out, gmix, gw, gb = pl.pallas_call(
        functools.partial(kernel, n_row, n_col, row_tiles, col_tiles),
        out_shape=(
            jax.ShapeDtypeStruct((share, width), BF16),
            jax.ShapeDtypeStruct((share, width), BF16),
            jax.ShapeDtypeStruct((n_col, chunk, width), gw_type),
            jax.ShapeDtypeStruct((n_row, 8, width), F32),
        ),
        in_specs=[anywhere] * 6 + [smem, anywhere],
        out_specs=(anywhere, vmem, anywhere, anywhere),
        scratch_shapes=[pltpu.VMEM(shape, kind) for shape, kind in buffers] + [
            pltpu.SMEM((index_rows, slots), jnp.int32),
            dma((CHUNKS,)), dma(()), dma((5 + PARTS,)), dma((3,)),
            row_sem, row_sem, chip_sem, chip_sem, chip_sem, chip_sem, chip_sem, chip_sem,
            chip_sem, chip_sem, row_sem, row_sem,
            col_sem, col_sem, row_sem, row_sem, col_sem, col_sem, row_sem, row_sem,
        ],
        compiler_params=pltpu.CompilerParams(
            collective_id=0, has_side_effects=True,
            vmem_limit_bytes=VMEM_BYTES),
        cost_estimate=pl.CostEstimate(
            flops=4 * row_tiles * col_tiles * side * side * width,
            bytes_accessed=2 * slots * side * side, transcendentals=share * width),
    )(features, weight, bias[None, :], grad_out, tile_rows[0], tile_cols[0], tile_counts, values)
    out, gfeat, gw, gb = pl.pallas_call(
        finish,
        out_shape=(
            jax.ShapeDtypeStruct((share, width), BF16),
            jax.ShapeDtypeStruct((share, width), BF16),
            jax.ShapeDtypeStruct((width, width), F32),
            jax.ShapeDtypeStruct((1, width), F32),
        ),
        in_specs=[vmem] * 5,
        out_specs=(vmem, vmem, vmem, vmem),
        compiler_params=pltpu.CompilerParams(vmem_limit_bytes=VMEM_BYTES),
    )(out, gmix, gw, gb, weight)
    return out, gfeat, gw, gb[0]


def solution(mesh):
    placed = (
        P(("col", "row"), None),
        P(),
        P(),
        P(("row", "col"), None),
        P("row", "col", None),
        P("row", "col", None),
        P("row", "col"),
        P("row", "col", None, None, None),
    )
    return jax.shard_map(
        functools.partial(body, mesh.shape["row"], mesh.shape["col"]),
        mesh=mesh,
        in_specs=placed,
        out_specs=(P(("row", "col"), None), P(("col", "row"), None), P(), P()),
        check_vma=False,
    )
```
